32 devices in a mesh: groups: 2 (over y), vocab: 8 (over z, x), mp: 2 (over core).
Axes of the slice: x: 2, y: 2, z: 4, core: 2. Of those that a mesh axis runs over, the one named last changes fastest.
Arguments:
- gate_pre: bfloat16 [32, 14336], P(('groups', 'vocab'), 'mp'), parts along dimension 0, may hold values from -6 to 6
- up_pre: bfloat16 [32, 14336], P(('groups', 'vocab'), 'mp'), parts along dimension 0, may hold values from -6 to 6
- down_weight: bfloat16 [8192, 14336], P('vocab', 'mp'), may hold values from -0.046875 to 0.046875
- residual: bfloat16 [32, 8192], P(('groups', 'vocab', 'mp')), parts along dimension 0, may hold values from -36 to 36
- norm_gain: bfloat16 [8192], replicated, may hold values from 0.5 to 1.5
- head_weight: bfloat16 [8192, 4032], P('mp', 'vocab')
- targets: int32 [32], P(('groups', 'mp')), parts along dimension 0, may hold values from 0 to 4031
Outputs:
- log_likelihood: float32 [32], P(('groups', 'mp')), parts along dimension 0
The draws below stay inside these ranges and needn't reach their ends.
There are 2 independent parts, one for each index of `groups`. The reference program is written for one: setup_inputs(seed, part) draws one part's arguments, and reference() takes and returns one part's arrays. A program takes and returns all parts, laid end to end along the dimension named above; an argument that names none is the same for every part. Nothing has to cross between parts.
All inputs are finite; a program needn't handle non-finite values.
Results may differ from the reference program's by a relative error of at most 0.0003.
The reference program's roundings to bfloat16 on the way (of `gated_units`, `stream` and `normed`) count: a program that leaves them out, or rounds other values in their place, can miss the bound.
Values may be sent and summed in bfloat16 or wider, within the bound.
A program may use at most 64 MiB of HBM per device.

```python
import math
import jax
import jax.numpy as jnp
from jax import lax

D = 8192
FF = 14336
TOKENS = 16
VOCAB = 4032


def draw_residual(key, part):
    subkeys = jax.random.split(key, 3)
    row_scale = jnp.exp(jax.random.uniform(subkeys[0], (TOKENS, 1), jnp.float32, math.log(0.3), math.log(3.0)))
    column_scale = jnp.exp(jax.random.uniform(subkeys[1], (1, D), jnp.float32, math.log(0.3), math.log(3.0)))
    rough_part = jnp.clip(jax.random.normal(subkeys[2], (TOKENS, D), jnp.float32), -4.0, 4.0)
    return (rough_part * row_scale * column_scale).astype(jnp.bfloat16)


def draw_head_weight(key, part):
    subkeys = jax.random.split(key, 2)
    rising = 1.2 + 1.2 * jnp.arange(VOCAB, dtype=jnp.float32) / VOCAB
    spread = jnp.exp(jax.random.uniform(subkeys[1], (VOCAB,), jnp.float32, 0.0, math.log(3.0)))
    scales = (spread * rising)[None, :] / math.sqrt(D)
    noise_draw = jnp.clip(jax.random.normal(subkeys[0], (D, VOCAB), jnp.float32), -4.0, 4.0)
    return (noise_draw * scales).astype(jnp.bfloat16)


def with_ends(drawn, key, low, largest):
    place = [jax.random.randint(jax.random.fold_in(key, axis), (), 0, length) for axis, length in enumerate(drawn.shape)]
    longest = drawn.shape.index(max(drawn.shape))
    beside = place[:longest] + [(place[longest] + 1) % drawn.shape[longest]] + place[longest + 1:]
    return drawn.at[tuple(place)].set(low).at[tuple(beside)].set(largest)


def steps_of(rng, extent, cuts, low, top_value):
    level = 1.0
    for dim, shards_of in cuts:
        steps = jax.random.uniform(jax.random.fold_in(jax.random.fold_in(rng, 6), dim), (shards_of,), jnp.float32, low / len(cuts), top_value / len(cuts))
        level = level * jnp.repeat(jnp.exp(steps), extent[dim] // shards_of).reshape((-1,) + (1,) * (len(extent) - 1 - dim))
    return level


def normal_values(stream_key, extent, width, reach, shards=(), held_as=jnp.bfloat16):
    values = width * jax.random.normal(stream_key, extent, jnp.float32)
    if shards:
        values = values * steps_of(stream_key, extent, shards, -0.22, 0.18)
    return jnp.clip(values, -reach, reach).astype(held_as)


def setup_inputs(seed: int = 0, part: int = 0) -> dict:
    key_list = jax.random.split(jax.random.key(seed), 8)
    own_keys = jax.random.split(jax.random.fold_in(key_list[7], part), 8)
    gate_pre = normal_values(own_keys[0], (TOKENS, FF), 1.0, 6.0, ((0, 8), (1, 2)))
    up_pre = normal_values(own_keys[1], (TOKENS, FF), 1.0, 6.0, ((0, 8), (1, 2)))
    down_weight = normal_values(key_list[2], (D, FF), FF ** -0.5, 0.046875, ((0, 8), (1, 2)))
    residual = draw_residual(jax.random.fold_in(jax.random.fold_in(key_list[7], part), 71), part)
    norm_gain = jnp.clip(1.0 + 0.1 * jax.random.normal(key_list[4], (D,), jnp.float32), 0.5, 1.5).astype(jnp.bfloat16)
    head_weight = draw_head_weight(jax.random.fold_in(key_list[7], 71), part)
    targets = with_ends(jax.random.randint(own_keys[6], (TOKENS,), 0, VOCAB), jax.random.fold_in(own_keys[6], 1), 0, VOCAB - 1).astype(jnp.int32)
    return {"gate_pre": gate_pre, "up_pre": up_pre, "down_weight": down_weight, "residual": residual, "norm_gain": norm_gain, "head_weight": head_weight, "targets": targets}


def reference(gate_pre, up_pre, down_weight, residual, norm_gain, head_weight, targets):
    gated_units = (jax.nn.silu(gate_pre.astype(jnp.float32)) * up_pre.astype(jnp.float32)).astype(jnp.bfloat16)
    update = lax.dot_general(gated_units, down_weight, (((1,), (1,)), ((), ())), preferred_element_type=jnp.float32)
    stream = (residual.astype(jnp.float32) + update).astype(jnp.bfloat16)
    stream = lax.optimization_barrier(stream)
    widened = stream.astype(jnp.float32)
    mean_square = lax.optimization_barrier(jnp.mean(widened * widened, axis=1, keepdims=True))
    normed = (widened * lax.rsqrt(mean_square + 1e-05) * norm_gain.astype(jnp.float32)[None, :]).astype(jnp.bfloat16)
    logits = jnp.dot(normed, head_weight, preferred_element_type=jnp.float32)
    row_top = lax.optimization_barrier(jnp.max(logits, axis=1))
    exp_total = lax.optimization_barrier(jnp.sum(jnp.exp(logits - row_top[:, None]), axis=1))
    columns = lax.broadcasted_iota(jnp.int32, logits.shape, 1)
    chosen = lax.optimization_barrier(jnp.sum(jnp.where(columns == targets.astype(jnp.int32)[:, None], logits, 0.0), axis=1))
    return chosen - row_top - jnp.log(exp_total)
```

```python
import functools

import jax
import jax.numpy as jnp
from jax import lax
from jax.experimental import pallas as pl
from jax.experimental.pallas import tpu as pltpu
from jax.sharding import PartitionSpec as P

EPSILON = 1e-05


def merged_2(value, axis, combine):
    everything = jax.tree.map(lambda part: lax.all_gather(part, axis), value)
    first = jax.tree.map(lambda part: part[0], everything)

    def turn(k, so_far):
        return combine(so_far, jax.tree.map(lambda part: part[k], everything))

    return lax.fori_loop(1, lax.axis_size(axis), turn, first)


def merge_stats(earlier, follows):
    joint_max = jnp.maximum(earlier[0], follows[0])
    joint_sum = earlier[1] * jnp.exp(earlier[0] - joint_max) + follows[1] * jnp.exp(
        follows[0] - joint_max
    )
    return (joint_max, joint_sum, earlier[2] + follows[2])


def plain_body(gate_pre, up_pre, down_weight, residual, norm_gain, head_weight, targets):
    vocab_count = lax.axis_size("vocab")
    model_count = lax.axis_size("mp")
    model_index = lax.axis_index("mp")
    vocab_index = lax.axis_index("vocab")
    gated_units = (jax.nn.silu(gate_pre.astype(jnp.float32)) * up_pre.astype(jnp.float32)).astype(
        jnp.bfloat16
    )
    down_terms = lax.dot_general(
        lax.all_gather(gated_units, "vocab", axis=0, tiled=True),
        down_weight,
        (((1,), (1,)), ((), ())),
        preferred_element_type=jnp.float32,
    )
    own_rows = residual.shape[0]
    block_cols = down_weight.shape[0]
    grouped = down_terms.reshape(vocab_count, model_count, own_rows, block_cols)
    arrived = lax.all_to_all(
        lax.all_to_all(grouped, "vocab", split_axis=0, concat_axis=3, tiled=True),
        "mp",
        split_axis=1,
        concat_axis=0,
        tiled=True,
    )
    update = jnp.sum(arrived, axis=(0, 1))
    stream = (residual.astype(jnp.float32) + update).astype(jnp.bfloat16)
    stream = lax.optimization_barrier(stream)
    widened = stream.astype(jnp.float32)
    mean_square = jnp.mean(widened * widened, axis=1, keepdims=True)
    normed = (
        widened * lax.rsqrt(mean_square + EPSILON) * norm_gain.astype(jnp.float32)[None, :]
    ).astype(jnp.bfloat16)
    half_width = head_weight.shape[0]
    halves = lax.dynamic_slice_in_dim(
        lax.all_gather(normed, ("vocab", "mp"), axis=0, tiled=True),
        model_index * half_width,
        half_width,
        1,
    )
    logit_terms = jnp.dot(halves, head_weight, preferred_element_type=jnp.float32)
    logits = lax.psum_scatter(logit_terms, "mp", scatter_dimension=0, tiled=True)
    local_ids = targets - vocab_index * logits.shape[1]
    columns = lax.broadcasted_iota(jnp.int32, logits.shape, 1)
    chosen = jnp.sum(jnp.where(columns == local_ids[:, None], logits, 0.0), axis=1)
    row_top = jnp.max(logits, axis=1)
    exp_total = jnp.sum(jnp.exp(logits - row_top[:, None]), axis=1)
    merged = merged_2((row_top, exp_total, chosen), "vocab", merge_stats)
    return merged[2] - merged[0] - jnp.log(merged[1])


GATHER_CHUNKS = 2
WEIGHT_COLS = 512
LANES = 128


def diagonal(rows):
    return lax.broadcasted_iota(jnp.int32, (rows, LANES), 0) == lax.broadcasted_iota(
        jnp.int32, (rows, LANES), 1
    )


def to_lanes(column):
    rows = column.shape[0]
    spread = jnp.where(diagonal(rows), jnp.broadcast_to(column, (rows, LANES)), 0.0)
    return jnp.sum(spread, axis=0, keepdims=True)


def to_rows(lanes, rows):
    spread = jnp.where(diagonal(rows), jnp.broadcast_to(lanes, (rows, LANES)), 0.0)
    return jnp.sum(spread, axis=1, keepdims=True)


def kernel(
    V,
    M,
    targets_ref,
    gate_hbm,
    up_hbm,
    down_hbm,
    residual_hbm,
    gain_hbm,
    head_hbm,
    out_ref,
    gate,
    up,
    down,
    own_residual,
    gain,
    head,
    gated_in,
    gated_rows,
    gated,
    residual_out,
    residual_in,
    residual_rows,
    update_out,
    update_in,
    stream_out,
    stream_in,
    square_in,
    logits_out,
    logits_in,
    stats_in,
    in_sem,
    down_sem,
    gated_send,
    gated_recv,
    residual_send,
    residual_recv,
    update_sem,
    stream_send,
    stream_recv,
    square_send,
    square_recv,
    logits_sem,
    stats_send,
    stats_recv,
):
    v = lax.axis_index("vocab")
    m = lax.axis_index("mp")
    other = 1 - m
    me = v * M + m
    N = V * M
    token_rows, width = gate.shape
    T = V * token_rows
    block_cols = down.shape[1]
    part_cols = block_cols // M
    weight_chunks, _, weight_cols = down.shape
    chunks = gated_in.shape[0]
    chunk_cols = width // chunks
    own_tokens = T // M
    vocab_cols = head.shape[1]
    half_owner = v // (V // M)

    def peer(i):
        return lax.rem(me + i, N)

    def coords(index):
        return {"vocab": index // M, "mp": lax.rem(index, M)}

    def remote(src, dst, send, recv, vocab, mp):
        return pltpu.make_async_remote_copy(
            src_ref=src,
            dst_ref=dst,
            send_sem=send,
            recv_sem=recv,
            device_id={"vocab": vocab, "mp": mp},
            device_id_type=pl.DeviceIdType.MESH,
        )

    barrier = pltpu.get_barrier_semaphore()
    for i in range(1, N):
        pl.semaphore_signal(
            barrier, inc=1, device_id=coords(peer(i)), device_id_type=pl.DeviceIdType.MESH
        )

    loads = [
        pltpu.make_async_copy(gate_hbm, gate, in_sem.at[0]),
        pltpu.make_async_copy(up_hbm, up, in_sem.at[1]),
        pltpu.make_async_copy(residual_hbm, own_residual, in_sem.at[2]),
        pltpu.make_async_copy(gain_hbm, gain, in_sem.at[3]),
        pltpu.make_async_copy(head_hbm, head, in_sem.at[4]),
    ]
    for load in loads[:3]:
        load.start()

    def down_copy(k):
        return pltpu.make_async_copy(
            down_hbm.at[:, pl.ds(pl.multiple_of(k * weight_cols, weight_cols), weight_cols)],
            down.at[k],
            down_sem.at[k],
        )

    for k in range(weight_chunks):
        down_copy(k).start()
    loads[4].start()
    loads[3].start()

    loads[0].wait()
    loads[1].wait()
    for a in range(chunks):
        part = slice(a * chunk_cols, (a + 1) * chunk_cols)
        g = gate[:, part].astype(jnp.float32)
        u = up[:, part].astype(jnp.float32)
        gated_in[a, v] = (jax.nn.silu(g) * u).astype(jnp.bfloat16)
    loads[2].wait()
    for n in range(N):
        residual_out[n] = own_residual[:, n * part_cols : (n + 1) * part_cols].astype(jnp.float32)
    residual_in[me] = residual_out[me]

    pl.semaphore_wait(barrier, N - 1)

    def gated_copy(a, i):
        to = lax.rem(v + i, V)
        return remote(
            gated_in.at[a, v], gated_in.at[a, v], gated_send.at[a, i], gated_recv.at[a, v], to, m
        )

    def gated_arrival(a, i):
        source = lax.rem(v + i, V)
        return remote(
            gated_in.at[a, source],
            gated_in.at[a, source],
            gated_send.at[a, i],
            gated_recv.at[a, source],
            source,
            m,
        )

    def residual_copy(i):
        to = peer(i)
        return remote(
            residual_out.at[to],
            residual_in.at[me],
            residual_send.at[i],
            residual_recv.at[me],
            to // M,
            lax.rem(to, M),
        )

    def residual_arrival(i):
        source = peer(i)
        return remote(
            residual_out.at[source],
            residual_in.at[source],
            residual_send.at[i],
            residual_recv.at[source],
            source // M,
            lax.rem(source, M),
        )

    for a in range(chunks):
        for i in range(1, V):
            gated_copy(a, i).start()
    for i in range(1, N):
        residual_copy(i).start()

    per_chunk = weight_chunks // chunks

    def take_chunk(a):
        for i in range(1, V):
            gated_arrival(a, i).wait_recv()
        for s in range(V):
            gated_rows[s * token_rows : (s + 1) * token_rows, :] = gated_in[a, s].astype(
                jnp.float32
            )
        for k in range(per_chunk):
            gated[a * per_chunk + k] = gated_rows[
                :, k * weight_cols : (k + 1) * weight_cols
            ].astype(jnp.bfloat16)

    def term(k, which):
        rows = pl.ds(pl.multiple_of(which * part_cols, part_cols), part_cols)
        return lax.dot_general(
            gated[k],
            down[k, rows, :],
            (((1,), (1,)), ((), ())),
            preferred_element_type=jnp.float32,
        )

    zero = jnp.zeros((T, part_cols), jnp.float32)

    def both(k, sums):
        down_copy(k).wait()
        return sums[0] + term(k, other), sums[1] + term(k, m)

    def first(k, total):
        down_copy(k).wait()
        return total + term(k, other)

    sums = (zero, zero)
    for a in range(chunks - 1):
        take_chunk(a)
        sums = lax.fori_loop(a * per_chunk, (a + 1) * per_chunk, both, sums)
    take_chunk(chunks - 1)
    last = (chunks - 1) * per_chunk
    update_out[...] = lax.fori_loop(last, weight_chunks, first, sums[0])
    swap = remote(update_out, update_in, update_sem.at[0], update_sem.at[1], v, other)
    swap.start()
    own = lax.fori_loop(last, weight_chunks, lambda k, total: total + term(k, m), sums[1])

    for i in range(1, N):
        residual_arrival(i).wait_recv()
    for n in range(N):
        residual_rows[n : n + 1, :] = residual_in[n]
    swap.wait_recv()
    stream = (residual_rows[...] + (own + update_in[...])).astype(jnp.bfloat16)
    stream_out[...] = stream
    wide = stream.astype(jnp.float32)
    square_in[me] = to_lanes(jnp.sum(wide * wide, axis=1, keepdims=True))

    slot = lax.rem(v, V // M) * M + m

    def square_copy(i):
        to = peer(i)
        return remote(
            square_in.at[me],
            square_in.at[me],
            square_send.at[i],
            square_recv.at[me],
            to // M,
            lax.rem(to, M),
        )

    def square_arrival(i):
        source = peer(i)
        return remote(
            square_in.at[source],
            square_in.at[source],
            square_send.at[i],
            square_recv.at[source],
            source // M,
            lax.rem(source, M),
        )

    def stream_copy(i):
        return remote(
            stream_out,
            stream_in.at[slot],
            stream_send.at[i],
            stream_recv.at[slot],
            lax.rem(v + i, V),
            half_owner,
        )

    def stream_arrival(j):
        return remote(
            stream_out, stream_in.at[j], stream_send.at[0], stream_recv.at[j], v, other
        )

    for i in range(1, V):
        stream_copy(i).start()

    @pl.when(m != half_owner)
    def _():
        stream_copy(0).start()

    for i in range(1, N):
        square_copy(i).start()

    @pl.when(m == half_owner)
    def _():
        stream_in[slot] = stream

    loads[3].wait()
    loads[4].wait()
    for i in range(1, N):
        square_arrival(i).wait_recv()
    squares = square_in[0]
    for n in range(1, N):
        squares = squares + square_in[n]
    mean_square = to_rows(squares, T) * (1.0 / (N * part_cols))
    scale = lax.rsqrt(mean_square + EPSILON)

    slots = stream_in.shape[0]
    partial = jnp.zeros((T, vocab_cols), jnp.float32)
    for j in range(slots):

        @pl.when(jnp.logical_or(m != half_owner, slot != j))
        def _():
            stream_arrival(j).wait_recv()

        feature = pl.multiple_of(m * (slots * part_cols) + j * part_cols, part_cols)
        normed = (
            stream_in[j].astype(jnp.float32)
            * scale
            * gain[:, pl.ds(feature, part_cols)].astype(jnp.float32)
        ).astype(jnp.bfloat16)
        partial = partial + jnp.dot(
            normed,
            head[j * part_cols : (j + 1) * part_cols, :],
            preferred_element_type=jnp.float32,
        )

    for n in range(M):
        logits_out[n] = partial[n * own_tokens : (n + 1) * own_tokens, :]
    swap_logits = remote(
        logits_out.at[other], logits_in, logits_sem.at[0], logits_sem.at[1], v, other
    )
    swap_logits.start()
    row = lax.broadcasted_iota(jnp.int32, (own_tokens, vocab_cols), 0)
    wanted = jnp.zeros((own_tokens, vocab_cols), jnp.int32)
    for t in range(own_tokens):
        wanted = jnp.where(row == t, targets_ref[t], wanted)
    columns = lax.broadcasted_iota(jnp.int32, (own_tokens, vocab_cols), 1) + v * vocab_cols
    swap_logits.wait_recv()
    logits = logits_out[m] + logits_in[...]
    top = jnp.max(logits, axis=1, keepdims=True)
    total = jnp.sum(jnp.exp(logits - top), axis=1, keepdims=True)
    chosen = jnp.sum(jnp.where(columns == wanted, logits, 0.0), axis=1, keepdims=True)
    stats_in[v, :, 0:LANES] = to_lanes(top)
    stats_in[v, :, LANES : 2 * LANES] = to_lanes(total)
    stats_in[v, :, 2 * LANES : 3 * LANES] = to_lanes(chosen)

    def stats_copy(i):
        return remote(
            stats_in.at[v],
            stats_in.at[v],
            stats_send.at[i],
            stats_recv.at[v],
            lax.rem(v + i, V),
            m,
        )

    def stats_arrival(i):
        source = lax.rem(v + i, V)
        return remote(
            stats_in.at[source],
            stats_in.at[source],
            stats_send.at[i],
            stats_recv.at[source],
            source,
            m,
        )

    for i in range(1, V):
        stats_copy(i).start()
    for a in range(chunks):
        for i in range(1, V):
            gated_copy(a, i).wait_send()
    for i in range(1, N):
        residual_copy(i).wait_send()
        square_copy(i).wait_send()
    for i in range(1, V):
        stream_copy(i).wait_send()

    @pl.when(m != half_owner)
    def _():
        stream_copy(0).wait_send()

    swap.wait_send()
    swap_logits.wait_send()
    for i in range(1, V):
        stats_arrival(i).wait_recv()
    joint = stats_in[0, :, 0:LANES]
    for n in range(1, V):
        joint = jnp.maximum(joint, stats_in[n, :, 0:LANES])
    exp_total = jnp.zeros((1, LANES), jnp.float32)
    picked = jnp.zeros((1, LANES), jnp.float32)
    for n in range(V):
        exp_total = exp_total + stats_in[n, :, LANES : 2 * LANES] * jnp.exp(
            stats_in[n, :, 0:LANES] - joint
        )
        picked = picked + stats_in[n, :, 2 * LANES : 3 * LANES]
    out_ref[...] = picked - joint - jnp.log(exp_total)
    for i in range(1, V):
        stats_copy(i).wait_send()


def body(gate_pre, up_pre, down_weight, residual, norm_gain, head_weight, targets):
    V = lax.axis_size("vocab")
    M = lax.axis_size("mp")
    token_rows, width = gate_pre.shape
    block_cols = down_weight.shape[0]
    half_width, vocab_cols = head_weight.shape
    T = V * token_rows
    fits = (
        M == 2
        and V % M == 0
        and T <= LANES
        and T % 16 == 0
        and residual.shape[0] == 1
        and block_cols % (M * LANES) == 0
        and width % (GATHER_CHUNKS * WEIGHT_COLS) == 0
    )
    if not fits:
        return plain_body(
            gate_pre, up_pre, down_weight, residual, norm_gain, head_weight, targets
        )
    N = V * M
    part_cols = block_cols // M
    weight_chunks = width // WEIGHT_COLS
    slots = V
    any_space = pl.BlockSpec(memory_space=pl.ANY)
    f32, bf16 = jnp.float32, jnp.bfloat16
    dma = pltpu.SemaphoreType.DMA
    result = pl.pallas_call(
        functools.partial(kernel, V, M),
        out_shape=jax.ShapeDtypeStruct((1, LANES), f32),
        in_specs=[pl.BlockSpec(memory_space=pltpu.SMEM)] + [any_space] * 6,
        out_specs=pl.BlockSpec(memory_space=pltpu.VMEM),
        scratch_shapes=[
            pltpu.VMEM((token_rows, width), bf16),
            pltpu.VMEM((token_rows, width), bf16),
            pltpu.VMEM((weight_chunks, block_cols, WEIGHT_COLS), bf16),
            pltpu.VMEM(residual.shape, bf16),
            pltpu.VMEM((1, norm_gain.shape[0]), bf16),
            pltpu.VMEM(head_weight.shape, bf16),
            pltpu.VMEM((GATHER_CHUNKS, V, token_rows, width // GATHER_CHUNKS), bf16),
            pltpu.VMEM((T, width // GATHER_CHUNKS), f32),
            pltpu.VMEM((weight_chunks, T, WEIGHT_COLS), bf16),
            pltpu.VMEM((N, 1, part_cols), f32),
            pltpu.VMEM((N, 1, part_cols), f32),
            pltpu.VMEM((T, part_cols), f32),
            pltpu.VMEM((T, part_cols), f32),
            pltpu.VMEM((T, part_cols), f32),
            pltpu.VMEM((T, part_cols), bf16),
            pltpu.VMEM((slots, T, part_cols), bf16),
            pltpu.VMEM((N, 1, LANES), f32),
            pltpu.VMEM((M, T // M, vocab_cols), f32),
            pltpu.VMEM((T // M, vocab_cols), f32),
            pltpu.VMEM((V, 1, 3 * LANES), f32),
            dma((5,)),
            dma((weight_chunks,)),
            dma((GATHER_CHUNKS, V)),
            dma((GATHER_CHUNKS, V)),
            dma((N,)),
            dma((N,)),
            dma((2,)),
            dma((V,)),
            dma((slots,)),
            dma((N,)),
            dma((N,)),
            dma((2,)),
            dma((V,)),
            dma((V,)),
        ],
        compiler_params=pltpu.CompilerParams(
            collective_id=0, has_side_effects=True, vmem_limit_bytes=56 * 1024 * 1024
        ),
        name="scored_head",
    )(
        targets,
        gate_pre,
        up_pre,
        down_weight,
        residual,
        norm_gain.reshape(1, -1),
        head_weight,
    )
    return result[0, : targets.shape[0]]


def solution(mesh):
    return jax.shard_map(
        body,
        mesh=mesh,
        in_specs=(
            P(("groups", "vocab"), "mp"),
            P(("groups", "vocab"), "mp"),
            P("vocab", "mp"),
            P(("groups", "vocab", "mp"), None),
            P(),
            P("mp", "vocab"),
            P(("groups", "mp")),
        ),
        out_specs=P(("groups", "mp")),
        check_vma=False,
    )
```

```python
import functools

import jax
import jax.numpy as jnp
from jax import lax
from jax.experimental import pallas as pl
from jax.experimental.pallas import tpu as pltpu
from jax.sharding import PartitionSpec as P

EPSILON = 1e-05


def merged_2(value, axis, combine):
    everything = jax.tree.map(lambda part: lax.all_gather(part, axis), value)
    first = jax.tree.map(lambda part: part[0], everything)

    def turn(k, so_far):
        return combine(so_far, jax.tree.map(lambda part: part[k], everything))

    return lax.fori_loop(1, lax.axis_size(axis), turn, first)


def merge_stats(earlier, follows):
    joint_max = jnp.maximum(earlier[0], follows[0])
    joint_sum = earlier[1] * jnp.exp(earlier[0] - joint_max) + follows[1] * jnp.exp(
        follows[0] - joint_max
    )
    return (joint_max, joint_sum, earlier[2] + follows[2])


def plain_body(gate_pre, up_pre, down_weight, residual, norm_gain, head_weight, targets):
    vocab_count = lax.axis_size("vocab")
    model_count = lax.axis_size("mp")
    model_index = lax.axis_index("mp")
    vocab_index = lax.axis_index("vocab")
    gated_units = (jax.nn.silu(gate_pre.astype(jnp.float32)) * up_pre.astype(jnp.float32)).astype(
        jnp.bfloat16
    )
    down_terms = lax.dot_general(
        lax.all_gather(gated_units, "vocab", axis=0, tiled=True),
        down_weight,
        (((1,), (1,)), ((), ())),
        preferred_element_type=jnp.float32,
    )
    own_rows = residual.shape[0]
    block_cols = down_weight.shape[0]
    grouped = down_terms.reshape(vocab_count, model_count, own_rows, block_cols)
    arrived = lax.all_to_all(
        lax.all_to_all(grouped, "vocab", split_axis=0, concat_axis=3, tiled=True),
        "mp",
        split_axis=1,
        concat_axis=0,
        tiled=True,
    )
    update = jnp.sum(arrived, axis=(0, 1))
    stream = (residual.astype(jnp.float32) + update).astype(jnp.bfloat16)
    stream = lax.optimization_barrier(stream)
    widened = stream.astype(jnp.float32)
    mean_square = jnp.mean(widened * widened, axis=1, keepdims=True)
    normed = (
        widened * lax.rsqrt(mean_square + EPSILON) * norm_gain.astype(jnp.float32)[None, :]
    ).astype(jnp.bfloat16)
    half_width = head_weight.shape[0]
    halves = lax.dynamic_slice_in_dim(
        lax.all_gather(normed, ("vocab", "mp"), axis=0, tiled=True),
        model_index * half_width,
        half_width,
        1,
    )
    logit_terms = jnp.dot(halves, head_weight, preferred_element_type=jnp.float32)
    logits = lax.psum_scatter(logit_terms, "mp", scatter_dimension=0, tiled=True)
    local_ids = targets - vocab_index * logits.shape[1]
    columns = lax.broadcasted_iota(jnp.int32, logits.shape, 1)
    chosen = jnp.sum(jnp.where(columns == local_ids[:, None], logits, 0.0), axis=1)
    row_top = jnp.max(logits, axis=1)
    exp_total = jnp.sum(jnp.exp(logits - row_top[:, None]), axis=1)
    merged = merged_2((row_top, exp_total, chosen), "vocab", merge_stats)
    return merged[2] - merged[0] - jnp.log(merged[1])


GATHER_CHUNKS = 4
MATRIX_SIDE = 256
LANES = 128


def diagonal(rows):
    return lax.broadcasted_iota(jnp.int32, (rows, LANES), 0) == lax.broadcasted_iota(
        jnp.int32, (rows, LANES), 1
    )


def to_lanes(column):
    rows = column.shape[0]
    spread = jnp.where(diagonal(rows), jnp.broadcast_to(column, (rows, LANES)), 0.0)
    return jnp.sum(spread, axis=0, keepdims=True)


def to_rows(lanes, rows):
    spread = jnp.where(diagonal(rows), jnp.broadcast_to(lanes, (rows, LANES)), 0.0)
    return jnp.sum(spread, axis=1, keepdims=True)


def kernel(
    V,
    M,
    targets_ref,
    gate_hbm,
    up_hbm,
    down_hbm,
    residual_hbm,
    gain_hbm,
    head_hbm,
    out_ref,
    gate,
    up,
    down,
    own_residual,
    gain,
    head,
    gated_in,
    gated_rows,
    residual_out,
    residual_in,
    residual_rows,
    update_out,
    update_in,
    stream_out,
    stream_in,
    square_in,
    logits_out,
    logits_in,
    stats_in,
    in_sem,
    down_sem,
    gated_send,
    gated_recv,
    residual_send,
    residual_recv,
    update_sem,
    stream_send,
    stream_recv,
    square_send,
    square_recv,
    logits_sem,
    stats_send,
    stats_recv,
):
    v = lax.axis_index("vocab")
    m = lax.axis_index("mp")
    other = 1 - m
    me = v * M + m
    N = V * M
    token_rows, width = gate.shape
    T = V * token_rows
    block_cols = down.shape[1]
    part_cols = block_cols // M
    chunks, _, chunk_cols = down.shape
    own_tokens = T // M
    vocab_cols = head.shape[0]
    half_owner = v // (V // M)

    def peer(i):
        return lax.rem(me + i, N)

    def coords(index):
        return {"vocab": index // M, "mp": lax.rem(index, M)}

    def remote(src, dst, send, recv, vocab, mp):
        return pltpu.make_async_remote_copy(
            src_ref=src,
            dst_ref=dst,
            send_sem=send,
            recv_sem=recv,
            device_id={"vocab": vocab, "mp": mp},
            device_id_type=pl.DeviceIdType.MESH,
        )

    barrier = pltpu.get_barrier_semaphore()
    for i in range(1, N):
        pl.semaphore_signal(
            barrier, inc=1, device_id=coords(peer(i)), device_id_type=pl.DeviceIdType.MESH
        )

    loads = [
        pltpu.make_async_copy(gate_hbm, gate, in_sem.at[0]),
        pltpu.make_async_copy(up_hbm, up, in_sem.at[1]),
        pltpu.make_async_copy(residual_hbm, own_residual, in_sem.at[2]),
        pltpu.make_async_copy(
            gain_hbm.at[pl.ds(pl.multiple_of(m * gain.shape[0], gain.shape[0]), gain.shape[0])],
            gain,
            in_sem.at[3],
        ),
        pltpu.make_async_copy(head_hbm, head, in_sem.at[4]),
    ]
    for load in loads[:3]:
        load.start()

    def down_copy(k):
        return pltpu.make_async_copy(
            down_hbm.at[:, pl.ds(pl.multiple_of(k * chunk_cols, chunk_cols), chunk_cols)],
            down.at[k],
            down_sem.at[k],
        )

    for k in range(chunks):
        down_copy(k).start()
    loads[4].start()
    loads[3].start()

    loads[0].wait()
    loads[1].wait()
    for a in range(chunks):
        part = slice(a * chunk_cols, (a + 1) * chunk_cols)
        g = gate[:, part].astype(jnp.float32)
        u = up[:, part].astype(jnp.float32)
        gated_in[a, v] = (jax.nn.silu(g) * u).astype(jnp.bfloat16)
    loads[2].wait()
    for n in range(N):
        residual_out[n] = own_residual[:, n * part_cols : (n + 1) * part_cols].astype(jnp.float32)
    residual_in[me] = residual_out[me]

    pl.semaphore_wait(barrier, N - 1)

    def gated_copy(a, i):
        to = lax.rem(v + i, V)
        return remote(
            gated_in.at[a, v], gated_in.at[a, v], gated_send.at[a, i], gated_recv.at[a, v], to, m
        )

    def gated_arrival(a, i):
        source = lax.rem(v + i, V)
        return remote(
            gated_in.at[a, source],
            gated_in.at[a, source],
            gated_send.at[a, i],
            gated_recv.at[a, source],
            source,
            m,
        )

    def residual_copy(i):
        to = peer(i)
        return remote(
            residual_out.at[to],
            residual_in.at[me],
            residual_send.at[i],
            residual_recv.at[me],
            to // M,
            lax.rem(to, M),
        )

    def residual_arrival(i):
        source = peer(i)
        return remote(
            residual_out.at[source],
            residual_in.at[source],
            residual_send.at[i],
            residual_recv.at[source],
            source // M,
            lax.rem(source, M),
        )

    for a in range(chunks):
        for i in range(1, V):
            gated_copy(a, i).start()
    for i in range(1, N):
        residual_copy(i).start()

    def take_chunk(a):
        for i in range(1, V):
            gated_arrival(a, i).wait_recv()
        for s in range(V):
            gated_rows[s * token_rows : (s + 1) * token_rows, :] = gated_in[a, s].astype(
                jnp.float32
            )
        return gated_rows[...].astype(jnp.bfloat16)

    def term(gated, a, which):
        rows = pl.ds(pl.multiple_of(which * part_cols, part_cols), part_cols)
        return lax.dot_general(
            gated,
            down[a, rows, :],
            (((1,), (1,)), ((), ())),
            preferred_element_type=jnp.float32,
        )

    theirs = jnp.zeros((T, part_cols), jnp.float32)
    own = theirs
    for a in range(chunks):
        gated = take_chunk(a)
        down_copy(a).wait()
        theirs = theirs + term(gated, a, other)
        if a == chunks - 1:
            update_out[...] = theirs
            swap = remote(update_out, update_in, update_sem.at[0], update_sem.at[1], v, other)
            swap.start()
        own = own + term(gated, a, m)

    for i in range(1, N):
        residual_arrival(i).wait_recv()
    for n in range(N):
        residual_rows[n : n + 1, :] = residual_in[n]
    swap.wait_recv()
    stream = (residual_rows[...] + (own + update_in[...])).astype(jnp.bfloat16)
    stream_out[...] = stream
    wide = stream.astype(jnp.float32)
    square_in[me] = to_lanes(jnp.sum(wide * wide, axis=1, keepdims=True))

    slot = lax.rem(v, V // M) * M + m

    def square_copy(i):
        to = peer(i)
        return remote(
            square_in.at[me],
            square_in.at[me],
            square_send.at[i],
            square_recv.at[me],
            to // M,
            lax.rem(to, M),
        )

    def square_arrival(i):
        source = peer(i)
        return remote(
            square_in.at[source],
            square_in.at[source],
            square_send.at[i],
            square_recv.at[source],
            source // M,
            lax.rem(source, M),
        )

    def stream_copy(i):
        return remote(
            stream_out,
            stream_in.at[slot],
            stream_send.at[i],
            stream_recv.at[slot],
            lax.rem(v + i, V),
            half_owner,
        )

    def stream_arrival(j):
        return remote(
            stream_out, stream_in.at[j], stream_send.at[0], stream_recv.at[j], v, other
        )

    for i in range(1, N):
        square_copy(i).start()
    for i in range(1, V):
        stream_copy(i).start()

    @pl.when(m != half_owner)
    def _():
        stream_copy(0).start()

    @pl.when(m == half_owner)
    def _():
        stream_in[slot] = stream

    loads[3].wait()
    loads[4].wait()
    for i in range(1, N):
        square_arrival(i).wait_recv()
    squares = square_in[0]
    for n in range(1, N):
        squares = squares + square_in[n]
    mean_square = to_rows(squares, T) * (1.0 / (N * part_cols))
    scale = lax.rsqrt(mean_square + EPSILON)

    slots = stream_in.shape[0]
    gains = gain[...].astype(jnp.float32)
    partial = jnp.zeros((T, vocab_cols), jnp.float32)
    for j in range(slots):

        @pl.when(jnp.logical_or(m != half_owner, slot != j))
        def _():
            stream_arrival(j).wait_recv()

        group = part_cols // LANES
        slot_gain = jnp.concatenate(
            [gains[j * group + q : j * group + q + 1] for q in range(group)], axis=1
        )
        normed = (
            stream_in[j].astype(jnp.float32)
            * scale
            * slot_gain
        ).astype(jnp.bfloat16)
        partial = partial + lax.dot_general(
            normed,
            head[:, j * part_cols : (j + 1) * part_cols],
            (((1,), (1,)), ((), ())),
            preferred_element_type=jnp.float32,
        )

    for n in range(M):
        logits_out[n] = partial[n * own_tokens : (n + 1) * own_tokens, :]
    swap_logits = remote(
        logits_out.at[other], logits_in, logits_sem.at[0], logits_sem.at[1], v, other
    )
    swap_logits.start()
    row = lax.broadcasted_iota(jnp.int32, (own_tokens, vocab_cols), 0)
    wanted = jnp.zeros((own_tokens, vocab_cols), jnp.int32)
    for t in range(own_tokens):
        wanted = jnp.where(row == t, targets_ref[t], wanted)
    columns = lax.broadcasted_iota(jnp.int32, (own_tokens, vocab_cols), 1) + v * vocab_cols
    swap_logits.wait_recv()
    logits = logits_out[m] + logits_in[...]
    top = jnp.max(logits, axis=1, keepdims=True)
    total = jnp.sum(jnp.exp(logits - top), axis=1, keepdims=True)
    chosen = jnp.sum(jnp.where(columns == wanted, logits, 0.0), axis=1, keepdims=True)
    stats_in[v, :, 0:LANES] = to_lanes(top)
    stats_in[v, :, LANES : 2 * LANES] = to_lanes(total)
    stats_in[v, :, 2 * LANES : 3 * LANES] = to_lanes(chosen)

    def stats_copy(i):
        return remote(
            stats_in.at[v],
            stats_in.at[v],
            stats_send.at[i],
            stats_recv.at[v],
            lax.rem(v + i, V),
            m,
        )

    def stats_arrival(i):
        source = lax.rem(v + i, V)
        return remote(
            stats_in.at[source],
            stats_in.at[source],
            stats_send.at[i],
            stats_recv.at[source],
            source,
            m,
        )

    for i in range(1, V):
        stats_copy(i).start()
    for a in range(chunks):
        for i in range(1, V):
            gated_copy(a, i).wait_send()
    for i in range(1, N):
        residual_copy(i).wait_send()
        square_copy(i).wait_send()
    for i in range(1, V):
        stream_copy(i).wait_send()

    @pl.when(m != half_owner)
    def _():
        stream_copy(0).wait_send()

    swap.wait_send()
    swap_logits.wait_send()
    for i in range(1, V):
        stats_arrival(i).wait_recv()
    joint = stats_in[0, :, 0:LANES]
    for n in range(1, V):
        joint = jnp.maximum(joint, stats_in[n, :, 0:LANES])
    exp_total = jnp.zeros((1, LANES), jnp.float32)
    picked = jnp.zeros((1, LANES), jnp.float32)
    for n in range(V):
        exp_total = exp_total + stats_in[n, :, LANES : 2 * LANES] * jnp.exp(
            stats_in[n, :, 0:LANES] - joint
        )
        picked = picked + stats_in[n, :, 2 * LANES : 3 * LANES]
    out_ref[...] = picked - joint - jnp.log(exp_total)
    for i in range(1, V):
        stats_copy(i).wait_send()


def body(gate_pre, up_pre, down_weight, residual, norm_gain, head_weight, targets):
    V = lax.axis_size("vocab")
    M = lax.axis_size("mp")
    token_rows, width = gate_pre.shape
    block_cols = down_weight.shape[0]
    half_width, vocab_cols = head_weight.shape
    T = V * token_rows
    fits = (
        M == 2
        and V % M == 0
        and T <= LANES
        and T % 16 == 0
        and residual.shape[0] == 1
        and block_cols % (M * LANES) == 0
        and width % (GATHER_CHUNKS * MATRIX_SIDE) == 0
        and half_width % (16 * LANES) == 0
    )
    if not fits:
        return plain_body(
            gate_pre, up_pre, down_weight, residual, norm_gain, head_weight, targets
        )
    N = V * M
    part_cols = block_cols // M
    chunk_cols = width // GATHER_CHUNKS
    slots = V
    any_space = pl.BlockSpec(memory_space=pl.ANY)
    f32, bf16 = jnp.float32, jnp.bfloat16
    dma = pltpu.SemaphoreType.DMA
    result = pl.pallas_call(
        functools.partial(kernel, V, M),
        out_shape=jax.ShapeDtypeStruct((1, LANES), f32),
        in_specs=[pl.BlockSpec(memory_space=pltpu.SMEM)] + [any_space] * 6,
        out_specs=pl.BlockSpec(memory_space=pltpu.VMEM),
        scratch_shapes=[
            pltpu.VMEM((token_rows, width), bf16),
            pltpu.VMEM((token_rows, width), bf16),
            pltpu.VMEM((GATHER_CHUNKS, block_cols, chunk_cols), bf16),
            pltpu.VMEM(residual.shape, bf16),
            pltpu.VMEM((half_width // LANES, LANES), bf16),
            pltpu.VMEM((vocab_cols, half_width), bf16),
            pltpu.VMEM((GATHER_CHUNKS, V, token_rows, chunk_cols), bf16),
            pltpu.VMEM((T, chunk_cols), f32),
            pltpu.VMEM((N, 1, part_cols), f32),
            pltpu.VMEM((N, 1, part_cols), f32),
            pltpu.VMEM((T, part_cols), f32),
            pltpu.VMEM((T, part_cols), f32),
            pltpu.VMEM((T, part_cols), f32),
            pltpu.VMEM((T, part_cols), bf16),
            pltpu.VMEM((slots, T, part_cols), bf16),
            pltpu.VMEM((N, 1, LANES), f32),
            pltpu.VMEM((M, T // M, vocab_cols), f32),
            pltpu.VMEM((T // M, vocab_cols), f32),
            pltpu.VMEM((V, 1, 3 * LANES), f32),
            dma((5,)),
            dma((GATHER_CHUNKS,)),
            dma((GATHER_CHUNKS, V)),
            dma((GATHER_CHUNKS, V)),
            dma((N,)),
            dma((N,)),
            dma((2,)),
            dma((V,)),
            dma((slots,)),
            dma((N,)),
            dma((N,)),
            dma((2,)),
            dma((V,)),
            dma((V,)),
        ],
        compiler_params=pltpu.CompilerParams(
            collective_id=0, has_side_effects=True, vmem_limit_bytes=56 * 1024 * 1024
        ),
        name="scored_head",
    )(
        targets,
        gate_pre,
        up_pre,
        down_weight,
        residual,
        norm_gain.reshape(-1, LANES),
        head_weight.T,
    )
    return result[0, : targets.shape[0]]


def solution(mesh):
    return jax.shard_map(
        body,
        mesh=mesh,
        in_specs=(
            P(("groups", "vocab"), "mp"),
            P(("groups", "vocab"), "mp"),
            P("vocab", "mp"),
            P(("groups", "vocab", "mp"), None),
            P(),
            P("mp", "vocab"),
            P(("groups", "mp")),
        ),
        out_specs=P(("groups", "mp")),
        check_vma=False,
    )
```

```python
import functools

import jax
import jax.numpy as jnp
from jax import lax
from jax.experimental import pallas as pl
from jax.experimental.pallas import tpu as pltpu
from jax.sharding import PartitionSpec as P

EPSILON = 1e-05


def merged_2(value, axis, combine):
    everything = jax.tree.map(lambda part: lax.all_gather(part, axis), value)
    first = jax.tree.map(lambda part: part[0], everything)

    def turn(k, so_far):
        return combine(so_far, jax.tree.map(lambda part: part[k], everything))

    return lax.fori_loop(1, lax.axis_size(axis), turn, first)


def merge_stats(earlier, follows):
    joint_max = jnp.maximum(earlier[0], follows[0])
    joint_sum = earlier[1] * jnp.exp(earlier[0] - joint_max) + follows[1] * jnp.exp(
        follows[0] - joint_max
    )
    return (joint_max, joint_sum, earlier[2] + follows[2])


def plain_body(gate_pre, up_pre, down_weight, residual, norm_gain, head_weight, targets):
    vocab_count = lax.axis_size("vocab")
    model_count = lax.axis_size("mp")
    model_index = lax.axis_index("mp")
    vocab_index = lax.axis_index("vocab")
    gated_units = (jax.nn.silu(gate_pre.astype(jnp.float32)) * up_pre.astype(jnp.float32)).astype(
        jnp.bfloat16
    )
    down_terms = lax.dot_general(
        lax.all_gather(gated_units, "vocab", axis=0, tiled=True),
        down_weight,
        (((1,), (1,)), ((), ())),
        preferred_element_type=jnp.float32,
    )
    own_rows = residual.shape[0]
    block_cols = down_weight.shape[0]
    grouped = down_terms.reshape(vocab_count, model_count, own_rows, block_cols)
    arrived = lax.all_to_all(
        lax.all_to_all(grouped, "vocab", split_axis=0, concat_axis=3, tiled=True),
        "mp",
        split_axis=1,
        concat_axis=0,
        tiled=True,
    )
    update = jnp.sum(arrived, axis=(0, 1))
    stream = (residual.astype(jnp.float32) + update).astype(jnp.bfloat16)
    stream = lax.optimization_barrier(stream)
    widened = stream.astype(jnp.float32)
    mean_square = jnp.mean(widened * widened, axis=1, keepdims=True)
    normed = (
        widened * lax.rsqrt(mean_square + EPSILON) * norm_gain.astype(jnp.float32)[None, :]
    ).astype(jnp.bfloat16)
    half_width = head_weight.shape[0]
    halves = lax.dynamic_slice_in_dim(
        lax.all_gather(normed, ("vocab", "mp"), axis=0, tiled=True),
        model_index * half_width,
        half_width,
        1,
    )
    logit_terms = jnp.dot(halves, head_weight, preferred_element_type=jnp.float32)
    logits = lax.psum_scatter(logit_terms, "mp", scatter_dimension=0, tiled=True)
    local_ids = targets - vocab_index * logits.shape[1]
    columns = lax.broadcasted_iota(jnp.int32, logits.shape, 1)
    chosen = jnp.sum(jnp.where(columns == local_ids[:, None], logits, 0.0), axis=1)
    row_top = jnp.max(logits, axis=1)
    exp_total = jnp.sum(jnp.exp(logits - row_top[:, None]), axis=1)
    merged = merged_2((row_top, exp_total, chosen), "vocab", merge_stats)
    return merged[2] - merged[0] - jnp.log(merged[1])


GATHER_CHUNKS = 4
MATRIX_SIDE = 256
LANES = 128


def diagonal(rows):
    return lax.broadcasted_iota(jnp.int32, (rows, LANES), 0) == lax.broadcasted_iota(
        jnp.int32, (rows, LANES), 1
    )


def to_lanes(column):
    rows = column.shape[0]
    spread = jnp.where(diagonal(rows), jnp.broadcast_to(column, (rows, LANES)), 0.0)
    return jnp.sum(spread, axis=0, keepdims=True)


def to_rows(lanes, rows):
    spread = jnp.where(diagonal(rows), jnp.broadcast_to(lanes, (rows, LANES)), 0.0)
    return jnp.sum(spread, axis=1, keepdims=True)


def kernel(
    V,
    M,
    targets_ref,
    gate_hbm,
    up_hbm,
    down_hbm,
    residual_hbm,
    gain_hbm,
    head_hbm,
    out_ref,
    gate,
    up,
    down,
    own_residual,
    gain,
    head,
    gated_in,
    gated_rows,
    residual_out,
    residual_in,
    residual_rows,
    update_out,
    update_in,
    stream_out,
    stream_in,
    square_in,
    logits_out,
    logits_in,
    stats_in,
    in_sem,
    down_sem,
    gated_send,
    gated_recv,
    residual_send,
    residual_recv,
    update_sem,
    stream_send,
    stream_recv,
    square_send,
    square_recv,
    logits_sem,
    stats_send,
    stats_recv,
):
    v = lax.axis_index("vocab")
    m = lax.axis_index("mp")
    other = 1 - m
    me = v * M + m
    N = V * M
    token_rows, width = gate.shape
    T = V * token_rows
    block_cols = down.shape[1]
    part_cols = block_cols // M
    chunks, _, chunk_cols = down.shape
    own_tokens = T // M
    vocab_cols = head.shape[0]
    half_owner = v // (V // M)

    def peer(i):
        return lax.rem(me + i, N)

    def coords(index):
        return {"vocab": index // M, "mp": lax.rem(index, M)}

    def remote(src, dst, send, recv, vocab, mp):
        return pltpu.make_async_remote_copy(
            src_ref=src,
            dst_ref=dst,
            send_sem=send,
            recv_sem=recv,
            device_id={"vocab": vocab, "mp": mp},
            device_id_type=pl.DeviceIdType.MESH,
        )

    barrier = pltpu.get_barrier_semaphore()
    for i in range(1, N):
        pl.semaphore_signal(
            barrier, inc=1, device_id=coords(peer(i)), device_id_type=pl.DeviceIdType.MESH
        )

    loads = [
        pltpu.make_async_copy(gate_hbm, gate, in_sem.at[0]),
        pltpu.make_async_copy(up_hbm, up, in_sem.at[1]),
        pltpu.make_async_copy(residual_hbm, own_residual, in_sem.at[2]),
        pltpu.make_async_copy(
            gain_hbm.at[pl.ds(pl.multiple_of(m * gain.shape[0], gain.shape[0]), gain.shape[0])],
            gain,
            in_sem.at[3],
        ),
        pltpu.make_async_copy(head_hbm, head, in_sem.at[4]),
    ]
    for load in loads[:3]:
        load.start()

    def down_copy(k):
        return pltpu.make_async_copy(
            down_hbm.at[:, pl.ds(pl.multiple_of(k * chunk_cols, chunk_cols), chunk_cols)],
            down.at[k],
            down_sem.at[k],
        )

    for k in range(chunks):
        down_copy(k).start()
    loads[4].start()
    loads[3].start()

    loads[0].wait()
    loads[1].wait()
    for a in range(chunks):
        part = slice(a * chunk_cols, (a + 1) * chunk_cols)
        g = gate[:, part].astype(jnp.float32)
        u = up[:, part].astype(jnp.float32)
        gated_in[a, v] = (jax.nn.silu(g) * u).astype(jnp.bfloat16)
    loads[2].wait()
    for n in range(N):
        residual_out[n] = own_residual[:, n * part_cols : (n + 1) * part_cols].astype(jnp.float32)
    residual_in[me] = residual_out[me]

    pl.semaphore_wait(barrier, N - 1)

    def gated_copy(a, i):
        to = lax.rem(v + i, V)
        return remote(
            gated_in.at[a, v], gated_in.at[a, v], gated_send.at[a, i], gated_recv.at[a, v], to, m
        )

    def gated_arrival(a, i):
        source = lax.rem(v + i, V)
        return remote(
            gated_in.at[a, source],
            gated_in.at[a, source],
            gated_send.at[a, i],
            gated_recv.at[a, source],
            source,
            m,
        )

    def residual_copy(i):
        to = peer(i)
        return remote(
            residual_out.at[to],
            residual_in.at[me],
            residual_send.at[i],
            residual_recv.at[me],
            to // M,
            lax.rem(to, M),
        )

    def residual_arrival(i):
        source = peer(i)
        return remote(
            residual_out.at[source],
            residual_in.at[source],
            residual_send.at[i],
            residual_recv.at[source],
            source // M,
            lax.rem(source, M),
        )

    for a in range(chunks):
        for i in range(1, V):
            gated_copy(a, i).start()
    for i in range(1, N):
        residual_copy(i).start()

    def take_chunk(a):
        for i in range(1, V):
            gated_arrival(a, i).wait_recv()
        for s in range(V):
            gated_rows[s * token_rows : (s + 1) * token_rows, :] = gated_in[a, s].astype(
                jnp.float32
            )
        return gated_rows[...].astype(jnp.bfloat16)

    def term(gated, a, which):
        rows = pl.ds(pl.multiple_of(which * part_cols, part_cols), part_cols)
        return lax.dot_general(
            down[a, rows, :],
            gated,
            (((1,), (1,)), ((), ())),
            preferred_element_type=jnp.float32,
        )

    theirs = jnp.zeros((part_cols, T), jnp.float32)
    own = theirs
    for a in range(chunks):
        gated = take_chunk(a)
        down_copy(a).wait()
        theirs = theirs + term(gated, a, other)
        if a == chunks - 1:
            update_out[...] = theirs.T
            swap = remote(update_out, update_in, update_sem.at[0], update_sem.at[1], v, other)
            swap.start()
        own = own + term(gated, a, m)

    for i in range(1, N):
        residual_arrival(i).wait_recv()
    for n in range(N):
        residual_rows[n : n + 1, :] = residual_in[n]
    swap.wait_recv()
    stream = (residual_rows[...] + (own.T + update_in[...])).astype(jnp.bfloat16)
    stream_out[...] = stream
    wide = stream.astype(jnp.float32)
    square_in[me] = to_lanes(jnp.sum(wide * wide, axis=1, keepdims=True))

    slot = lax.rem(v, V // M) * M + m

    def square_copy(i):
        to = peer(i)
        return remote(
            square_in.at[me],
            square_in.at[me],
            square_send.at[i],
            square_recv.at[me],
            to // M,
            lax.rem(to, M),
        )

    def square_arrival(i):
        source = peer(i)
        return remote(
            square_in.at[source],
            square_in.at[source],
            square_send.at[i],
            square_recv.at[source],
            source // M,
            lax.rem(source, M),
        )

    def stream_copy(i):
        return remote(
            stream_out,
            stream_in.at[slot],
            stream_send.at[i],
            stream_recv.at[slot],
            lax.rem(v + i, V),
            half_owner,
        )

    def stream_arrival(j):
        return remote(
            stream_out, stream_in.at[j], stream_send.at[0], stream_recv.at[j], v, other
        )

    for i in range(1, N):
        square_copy(i).start()
    for i in range(1, V):
        stream_copy(i).start()

    @pl.when(m != half_owner)
    def _():
        stream_copy(0).start()

    @pl.when(m == half_owner)
    def _():
        stream_in[slot] = stream

    loads[3].wait()
    loads[4].wait()
    for i in range(1, N):
        square_arrival(i).wait_recv()
    squares = square_in[0]
    for n in range(1, N):
        squares = squares + square_in[n]
    mean_square = to_rows(squares, T) * (1.0 / (N * part_cols))
    scale = lax.rsqrt(mean_square + EPSILON)

    slots = stream_in.shape[0]
    gains = gain[...].astype(jnp.float32)
    partial = jnp.zeros((vocab_cols, T), jnp.float32)
    for j in range(slots):

        @pl.when(jnp.logical_or(m != half_owner, slot != j))
        def _():
            stream_arrival(j).wait_recv()

        group = part_cols // LANES
        slot_gain = jnp.concatenate(
            [gains[j * group + q : j * group + q + 1] for q in range(group)], axis=1
        )
        normed = (
            stream_in[j].astype(jnp.float32)
            * scale
            * slot_gain
        ).astype(jnp.bfloat16)
        partial = partial + lax.dot_general(
            head[:, j * part_cols : (j + 1) * part_cols],
            normed,
            (((1,), (1,)), ((), ())),
            preferred_element_type=jnp.float32,
        )

    logits_t = partial.T
    for n in range(M):
        logits_out[n] = logits_t[n * own_tokens : (n + 1) * own_tokens, :]
    swap_logits = remote(
        logits_out.at[other], logits_in, logits_sem.at[0], logits_sem.at[1], v, other
    )
    swap_logits.start()
    row = lax.broadcasted_iota(jnp.int32, (own_tokens, vocab_cols), 0)
    wanted = jnp.zeros((own_tokens, vocab_cols), jnp.int32)
    for t in range(own_tokens):
        wanted = jnp.where(row == t, targets_ref[t], wanted)
    columns = lax.broadcasted_iota(jnp.int32, (own_tokens, vocab_cols), 1) + v * vocab_cols
    swap_logits.wait_recv()
    logits = logits_out[m] + logits_in[...]
    top = jnp.max(logits, axis=1, keepdims=True)
    total = jnp.sum(jnp.exp(logits - top), axis=1, keepdims=True)
    chosen = jnp.sum(jnp.where(columns == wanted, logits, 0.0), axis=1, keepdims=True)
    stats_in[v, :, 0:LANES] = to_lanes(top)
    stats_in[v, :, LANES : 2 * LANES] = to_lanes(total)
    stats_in[v, :, 2 * LANES : 3 * LANES] = to_lanes(chosen)

    def stats_copy(i):
        return remote(
            stats_in.at[v],
            stats_in.at[v],
            stats_send.at[i],
            stats_recv.at[v],
            lax.rem(v + i, V),
            m,
        )

    def stats_arrival(i):
        source = lax.rem(v + i, V)
        return remote(
            stats_in.at[source],
            stats_in.at[source],
            stats_send.at[i],
            stats_recv.at[source],
            source,
            m,
        )

    for i in range(1, V):
        stats_copy(i).start()
    for a in range(chunks):
        for i in range(1, V):
            gated_copy(a, i).wait_send()
    for i in range(1, N):
        residual_copy(i).wait_send()
        square_copy(i).wait_send()
    for i in range(1, V):
        stream_copy(i).wait_send()

    @pl.when(m != half_owner)
    def _():
        stream_copy(0).wait_send()

    swap.wait_send()
    swap_logits.wait_send()
    for i in range(1, V):
        stats_arrival(i).wait_recv()
    joint = stats_in[0, :, 0:LANES]
    for n in range(1, V):
        joint = jnp.maximum(joint, stats_in[n, :, 0:LANES])
    exp_total = jnp.zeros((1, LANES), jnp.float32)
    picked = jnp.zeros((1, LANES), jnp.float32)
    for n in range(V):
        exp_total = exp_total + stats_in[n, :, LANES : 2 * LANES] * jnp.exp(
            stats_in[n, :, 0:LANES] - joint
        )
        picked = picked + stats_in[n, :, 2 * LANES : 3 * LANES]
    out_ref[...] = picked - joint - jnp.log(exp_total)
    for i in range(1, V):
        stats_copy(i).wait_send()


def body(gate_pre, up_pre, down_weight, residual, norm_gain, head_weight, targets):
    V = lax.axis_size("vocab")
    M = lax.axis_size("mp")
    token_rows, width = gate_pre.shape
    block_cols = down_weight.shape[0]
    half_width, vocab_cols = head_weight.shape
    T = V * token_rows
    fits = (
        M == 2
        and V % M == 0
        and T <= LANES
        and T % 16 == 0
        and residual.shape[0] == 1
        and block_cols % (M * LANES) == 0
        and width % (GATHER_CHUNKS * MATRIX_SIDE) == 0
        and half_width % (16 * LANES) == 0
    )
    if not fits:
        return plain_body(
            gate_pre, up_pre, down_weight, residual, norm_gain, head_weight, targets
        )
    N = V * M
    part_cols = block_cols // M
    chunk_cols = width // GATHER_CHUNKS
    slots = V
    any_space = pl.BlockSpec(memory_space=pl.ANY)
    f32, bf16 = jnp.float32, jnp.bfloat16
    dma = pltpu.SemaphoreType.DMA
    result = pl.pallas_call(
        functools.partial(kernel, V, M),
        out_shape=jax.ShapeDtypeStruct((1, LANES), f32),
        in_specs=[pl.BlockSpec(memory_space=pltpu.SMEM)] + [any_space] * 6,
        out_specs=pl.BlockSpec(memory_space=pltpu.VMEM),
        scratch_shapes=[
            pltpu.VMEM((token_rows, width), bf16),
            pltpu.VMEM((token_rows, width), bf16),
            pltpu.VMEM((GATHER_CHUNKS, block_cols, chunk_cols), bf16),
            pltpu.VMEM(residual.shape, bf16),
            pltpu.VMEM((half_width // LANES, LANES), bf16),
            pltpu.VMEM((vocab_cols, half_width), bf16),
            pltpu.VMEM((GATHER_CHUNKS, V, token_rows, chunk_cols), bf16),
            pltpu.VMEM((T, chunk_cols), f32),
            pltpu.VMEM((N, 1, part_cols), f32),
            pltpu.VMEM((N, 1, part_cols), f32),
            pltpu.VMEM((T, part_cols), f32),
            pltpu.VMEM((T, part_cols), f32),
            pltpu.VMEM((T, part_cols), f32),
            pltpu.VMEM((T, part_cols), bf16),
            pltpu.VMEM((slots, T, part_cols), bf16),
            pltpu.VMEM((N, 1, LANES), f32),
            pltpu.VMEM((M, T // M, vocab_cols), f32),
            pltpu.VMEM((T // M, vocab_cols), f32),
            pltpu.VMEM((V, 1, 3 * LANES), f32),
            dma((5,)),
            dma((GATHER_CHUNKS,)),
            dma((GATHER_CHUNKS, V)),
            dma((GATHER_CHUNKS, V)),
            dma((N,)),
            dma((N,)),
            dma((2,)),
            dma((V,)),
            dma((slots,)),
            dma((N,)),
            dma((N,)),
            dma((2,)),
            dma((V,)),
            dma((V,)),
        ],
        compiler_params=pltpu.CompilerParams(
            collective_id=0, has_side_effects=True, vmem_limit_bytes=56 * 1024 * 1024
        ),
        name="scored_head",
    )(
        targets,
        gate_pre,
        up_pre,
        down_weight,
        residual,
        norm_gain.reshape(-1, LANES),
        head_weight.T,
    )
    return result[0, : targets.shape[0]]


def solution(mesh):
    return jax.shard_map(
        body,
        mesh=mesh,
        in_specs=(
            P(("groups", "vocab"), "mp"),
            P(("groups", "vocab"), "mp"),
            P("vocab", "mp"),
            P(("groups", "vocab", "mp"), None),
            P(),
            P("mp", "vocab"),
            P(("groups", "mp")),
        ),
        out_specs=P(("groups", "mp")),
        check_vma=False,
    )
```

```python
import functools

import jax
import jax.numpy as jnp
from jax import lax
from jax.experimental import pallas as pl
from jax.experimental.pallas import tpu as pltpu
from jax.sharding import PartitionSpec as P

EPSILON = 1e-05


def merged_2(value, axis, combine):
    everything = jax.tree.map(lambda part: lax.all_gather(part, axis), value)
    first = jax.tree.map(lambda part: part[0], everything)

    def turn(k, so_far):
        return combine(so_far, jax.tree.map(lambda part: part[k], everything))

    return lax.fori_loop(1, lax.axis_size(axis), turn, first)


def merge_stats(earlier, follows):
    joint_max = jnp.maximum(earlier[0], follows[0])
    joint_sum = earlier[1] * jnp.exp(earlier[0] - joint_max) + follows[1] * jnp.exp(
        follows[0] - joint_max
    )
    return (joint_max, joint_sum, earlier[2] + follows[2])


def plain_body(gate_pre, up_pre, down_weight, residual, norm_gain, head_weight, targets):
    vocab_count = lax.axis_size("vocab")
    model_count = lax.axis_size("mp")
    model_index = lax.axis_index("mp")
    vocab_index = lax.axis_index("vocab")
    gated_units = (jax.nn.silu(gate_pre.astype(jnp.float32)) * up_pre.astype(jnp.float32)).astype(
        jnp.bfloat16
    )
    down_terms = lax.dot_general(
        lax.all_gather(gated_units, "vocab", axis=0, tiled=True),
        down_weight,
        (((1,), (1,)), ((), ())),
        preferred_element_type=jnp.float32,
    )
    own_rows = residual.shape[0]
    block_cols = down_weight.shape[0]
    grouped = down_terms.reshape(vocab_count, model_count, own_rows, block_cols)
    arrived = lax.all_to_all(
        lax.all_to_all(grouped, "vocab", split_axis=0, concat_axis=3, tiled=True),
        "mp",
        split_axis=1,
        concat_axis=0,
        tiled=True,
    )
    update = jnp.sum(arrived, axis=(0, 1))
    stream = (residual.astype(jnp.float32) + update).astype(jnp.bfloat16)
    stream = lax.optimization_barrier(stream)
    widened = stream.astype(jnp.float32)
    mean_square = jnp.mean(widened * widened, axis=1, keepdims=True)
    normed = (
        widened * lax.rsqrt(mean_square + EPSILON) * norm_gain.astype(jnp.float32)[None, :]
    ).astype(jnp.bfloat16)
    half_width = head_weight.shape[0]
    halves = lax.dynamic_slice_in_dim(
        lax.all_gather(normed, ("vocab", "mp"), axis=0, tiled=True),
        model_index * half_width,
        half_width,
        1,
    )
    logit_terms = jnp.dot(halves, head_weight, preferred_element_type=jnp.float32)
    logits = lax.psum_scatter(logit_terms, "mp", scatter_dimension=0, tiled=True)
    local_ids = targets - vocab_index * logits.shape[1]
    columns = lax.broadcasted_iota(jnp.int32, logits.shape, 1)
    chosen = jnp.sum(jnp.where(columns == local_ids[:, None], logits, 0.0), axis=1)
    row_top = jnp.max(logits, axis=1)
    exp_total = jnp.sum(jnp.exp(logits - row_top[:, None]), axis=1)
    merged = merged_2((row_top, exp_total, chosen), "vocab", merge_stats)
    return merged[2] - merged[0] - jnp.log(merged[1])


GATHER_CHUNKS = 4
MATRIX_SIDE = 256
LANES = 128


def diagonal(rows):
    return lax.broadcasted_iota(jnp.int32, (rows, LANES), 0) == lax.broadcasted_iota(
        jnp.int32, (rows, LANES), 1
    )


def to_lanes(column):
    rows = column.shape[0]
    spread = jnp.where(diagonal(rows), jnp.broadcast_to(column, (rows, LANES)), 0.0)
    return jnp.sum(spread, axis=0, keepdims=True)


def to_rows(lanes, rows):
    spread = jnp.where(diagonal(rows), jnp.broadcast_to(lanes, (rows, LANES)), 0.0)
    return jnp.sum(spread, axis=1, keepdims=True)


def kernel(
    V,
    M,
    targets_ref,
    gate_hbm,
    up_hbm,
    down_hbm,
    residual_hbm,
    gain_hbm,
    head_hbm,
    out_ref,
    gate,
    up,
    down,
    own_residual,
    gain,
    gain_rows,
    head,
    gated_in,
    gated_rows,
    residual_out,
    residual_in,
    residual_rows,
    update_out,
    update_in,
    stream_out,
    stream_in,
    square_in,
    logits_out,
    logits_in,
    stats_in,
    in_sem,
    down_sem,
    gated_send,
    gated_recv,
    residual_send,
    residual_recv,
    update_sem,
    stream_send,
    stream_recv,
    square_send,
    square_recv,
    logits_sem,
    stats_send,
    stats_recv,
):
    v = lax.axis_index("vocab")
    m = lax.axis_index("mp")
    other = 1 - m
    me = v * M + m
    N = V * M
    token_rows, width = gate.shape
    T = V * token_rows
    block_cols = down.shape[1]
    part_cols = block_cols // M
    chunks, _, chunk_cols = down.shape
    own_tokens = T // M
    vocab_cols = head.shape[0]
    half_owner = v // (V // M)

    def peer(i):
        return lax.rem(me + i, N)

    def coords(index):
        return {"vocab": index // M, "mp": lax.rem(index, M)}

    def remote(src, dst, send, recv, vocab, mp):
        return pltpu.make_async_remote_copy(
            src_ref=src,
            dst_ref=dst,
            send_sem=send,
            recv_sem=recv,
            device_id={"vocab": vocab, "mp": mp},
            device_id_type=pl.DeviceIdType.MESH,
        )

    barrier = pltpu.get_barrier_semaphore()
    for i in range(1, N):
        pl.semaphore_signal(
            barrier, inc=1, device_id=coords(peer(i)), device_id_type=pl.DeviceIdType.MESH
        )

    loads = [
        pltpu.make_async_copy(gate_hbm, gate, in_sem.at[0]),
        pltpu.make_async_copy(up_hbm, up, in_sem.at[1]),
        pltpu.make_async_copy(residual_hbm, own_residual, in_sem.at[2]),
        pltpu.make_async_copy(
            gain_hbm.at[pl.ds(pl.multiple_of(m * gain.shape[0], gain.shape[0]), gain.shape[0])],
            gain,
            in_sem.at[3],
        ),
        pltpu.make_async_copy(head_hbm, head, in_sem.at[4]),
    ]
    for load in loads[:3]:
        load.start()

    def down_copy(k):
        return pltpu.make_async_copy(
            down_hbm.at[:, pl.ds(pl.multiple_of(k * chunk_cols, chunk_cols), chunk_cols)],
            down.at[k],
            down_sem.at[k],
        )

    for k in range(chunks):
        down_copy(k).start()
    loads[4].start()
    loads[3].start()

    def gated_copy(a, i):
        to = lax.rem(v + i, V)
        return remote(
            gated_in.at[a, v], gated_in.at[a, v], gated_send.at[a, i], gated_recv.at[a, v], to, m
        )

    def gated_arrival(a, i):
        source = lax.rem(v + i, V)
        return remote(
            gated_in.at[a, source],
            gated_in.at[a, source],
            gated_send.at[a, i],
            gated_recv.at[a, source],
            source,
            m,
        )

    def residual_copy(i):
        to = peer(i)
        return remote(
            residual_out.at[to],
            residual_in.at[me],
            residual_send.at[i],
            residual_recv.at[me],
            to // M,
            lax.rem(to, M),
        )

    def residual_arrival(i):
        source = peer(i)
        return remote(
            residual_out.at[source],
            residual_in.at[source],
            residual_send.at[i],
            residual_recv.at[source],
            source // M,
            lax.rem(source, M),
        )

    loads[0].wait()
    loads[1].wait()
    for a in range(chunks):
        part = slice(a * chunk_cols, (a + 1) * chunk_cols)
        g = gate[:, part].astype(jnp.float32)
        u = up[:, part].astype(jnp.float32)
        gated_in[a, v] = (jax.nn.silu(g) * u).astype(jnp.bfloat16)
        if a == 0:
            pl.semaphore_wait(barrier, N - 1)
        for i in range(1, V):
            gated_copy(a, i).start()
    loads[2].wait()
    for n in range(N):
        residual_out[n] = own_residual[:, n * part_cols : (n + 1) * part_cols].astype(jnp.float32)
    residual_in[me] = residual_out[me]
    for i in range(1, N):
        residual_copy(i).start()

    def await_chunk(a):
        for i in range(1, V):
            gated_arrival(a, i).wait_recv()
        down_copy(a).wait()

    def token_chunk(a):
        for s in range(V):
            gated_rows[a % 2, s * token_rows : (s + 1) * token_rows, :] = gated_in[a, s].astype(
                jnp.float32
            )
        return gated_rows[a % 2].astype(jnp.bfloat16)

    def term(gated, a, which):
        rows = pl.ds(pl.multiple_of(which * part_cols, part_cols), part_cols)
        return lax.dot_general(
            gated,
            down[a, rows, :],
            (((1,), (1,)), ((), ())),
            preferred_element_type=jnp.float32,
        )

    theirs = jnp.zeros((T, part_cols), jnp.float32)
    own = theirs
    await_chunk(0)
    gated = token_chunk(0)
    for a in range(chunks):
        theirs = theirs + term(gated, a, other)
        if a == chunks - 1:
            update_out[...] = theirs
            swap = remote(update_out, update_in, update_sem.at[0], update_sem.at[1], v, other)
            swap.start()
            own = own + term(gated, a, m)
        else:
            await_chunk(a + 1)
            following = token_chunk(a + 1)
            own = own + term(gated, a, m)
            gated = following

    loads[3].wait()
    loads[4].wait()
    group = part_cols // LANES
    gains = gain[...].astype(jnp.float32)
    for j in range(V):
        for q in range(group):
            gain_rows[j, :, q * LANES : (q + 1) * LANES] = gains[
                j * group + q : j * group + q + 1
            ]
    for i in range(1, N):
        residual_arrival(i).wait_recv()
    for n in range(N):
        residual_rows[n : n + 1, :] = residual_in[n]
    swap.wait_recv()
    stream = (residual_rows[...] + (own + update_in[...])).astype(jnp.bfloat16)
    stream_out[...] = stream
    wide = stream.astype(jnp.float32)
    square_in[me] = to_lanes(jnp.sum(wide * wide, axis=1, keepdims=True))

    slot = lax.rem(v, V // M) * M + m

    def square_copy(i):
        to = peer(i)
        return remote(
            square_in.at[me],
            square_in.at[me],
            square_send.at[i],
            square_recv.at[me],
            to // M,
            lax.rem(to, M),
        )

    def square_arrival(i):
        source = peer(i)
        return remote(
            square_in.at[source],
            square_in.at[source],
            square_send.at[i],
            square_recv.at[source],
            source // M,
            lax.rem(source, M),
        )

    quarter = V // M

    def stream_copy(i, h):
        to = lax.rem(v + i, quarter) + h * quarter
        return remote(
            stream_out,
            stream_in.at[slot],
            stream_send.at[h * quarter + i],
            stream_recv.at[slot],
            to,
            half_owner,
        )

    def over_stream(act):
        for i in range(quarter):
            for h in range(M):
                if i:
                    act(stream_copy(i, h))
                else:

                    @pl.when(jnp.logical_or(h != half_owner, m != half_owner))
                    def _():
                        act(stream_copy(i, h))

    def stream_arrival(j):
        return remote(
            stream_out, stream_in.at[j], stream_send.at[0], stream_recv.at[j], v, other
        )

    for i in range(1, N):
        square_copy(i).start()
    over_stream(lambda copy: copy.start())

    @pl.when(m == half_owner)
    def _():
        stream_in[slot] = stream

    for i in range(1, N):
        square_arrival(i).wait_recv()
    squares = square_in[0]
    for n in range(1, N):
        squares = squares + square_in[n]
    mean_square = to_rows(squares, T) * (1.0 / (N * part_cols))
    scale = lax.rsqrt(mean_square + EPSILON)

    partial = jnp.zeros((T, vocab_cols), jnp.float32)
    for i in range(quarter):
        source = lax.rem(v + quarter - i, quarter)
        for c in range(M):
            j = source * M + c
            if i:
                stream_arrival(j).wait_recv()
            else:

                @pl.when(jnp.logical_or(m != half_owner, m != c))
                def _():
                    stream_arrival(j).wait_recv()

            normed = (stream_in[j].astype(jnp.float32) * scale * gain_rows[j]).astype(
                jnp.bfloat16
            )
            features = pl.ds(pl.multiple_of(j * part_cols, part_cols), part_cols)
            partial = partial + lax.dot_general(
                normed,
                head[:, features],
                (((1,), (1,)), ((), ())),
                preferred_element_type=jnp.float32,
            )

    for n in range(M):
        logits_out[n] = partial[n * own_tokens : (n + 1) * own_tokens, :]
    swap_logits = remote(
        logits_out.at[other], logits_in, logits_sem.at[0], logits_sem.at[1], v, other
    )
    swap_logits.start()
    row = lax.broadcasted_iota(jnp.int32, (own_tokens, vocab_cols), 0)
    wanted = jnp.zeros((own_tokens, vocab_cols), jnp.int32)
    for t in range(own_tokens):
        wanted = jnp.where(row == t, targets_ref[t], wanted)
    columns = lax.broadcasted_iota(jnp.int32, (own_tokens, vocab_cols), 1) + v * vocab_cols
    swap_logits.wait_recv()
    logits = logits_out[m] + logits_in[...]
    top = jnp.max(logits, axis=1, keepdims=True)
    total = jnp.sum(jnp.exp(logits - top), axis=1, keepdims=True)
    chosen = jnp.sum(jnp.where(columns == wanted, logits, 0.0), axis=1, keepdims=True)
    stats_in[v, :, 0:LANES] = to_lanes(top)
    stats_in[v, :, LANES : 2 * LANES] = to_lanes(total)
    stats_in[v, :, 2 * LANES : 3 * LANES] = to_lanes(chosen)

    def stats_copy(i):
        return remote(
            stats_in.at[v],
            stats_in.at[v],
            stats_send.at[i],
            stats_recv.at[v],
            lax.rem(v + i, V),
            m,
        )

    def stats_arrival(i):
        source = lax.rem(v + i, V)
        return remote(
            stats_in.at[source],
            stats_in.at[source],
            stats_send.at[i],
            stats_recv.at[source],
            source,
            m,
        )

    for i in range(1, V):
        stats_copy(i).start()
    for a in range(chunks):
        for i in range(1, V):
            gated_copy(a, i).wait_send()
    for i in range(1, N):
        residual_copy(i).wait_send()
        square_copy(i).wait_send()
    over_stream(lambda copy: copy.wait_send())

    swap.wait_send()
    swap_logits.wait_send()
    for i in range(1, V):
        stats_arrival(i).wait_recv()
    joint = stats_in[0, :, 0:LANES]
    for n in range(1, V):
        joint = jnp.maximum(joint, stats_in[n, :, 0:LANES])
    exp_total = jnp.zeros((1, LANES), jnp.float32)
    picked = jnp.zeros((1, LANES), jnp.float32)
    for n in range(V):
        exp_total = exp_total + stats_in[n, :, LANES : 2 * LANES] * jnp.exp(
            stats_in[n, :, 0:LANES] - joint
        )
        picked = picked + stats_in[n, :, 2 * LANES : 3 * LANES]
    out_ref[...] = picked - joint - jnp.log(exp_total)
    for i in range(1, V):
        stats_copy(i).wait_send()


def body(gate_pre, up_pre, down_weight, residual, norm_gain, head_weight, targets):
    V = lax.axis_size("vocab")
    M = lax.axis_size("mp")
    token_rows, width = gate_pre.shape
    block_cols = down_weight.shape[0]
    half_width, vocab_cols = head_weight.shape
    T = V * token_rows
    fits = (
        M == 2
        and V % M == 0
        and T <= LANES
        and T % 16 == 0
        and residual.shape[0] == 1
        and block_cols % (M * LANES) == 0
        and width % (GATHER_CHUNKS * MATRIX_SIDE) == 0
        and half_width % (16 * LANES) == 0
    )
    if not fits:
        return plain_body(
            gate_pre, up_pre, down_weight, residual, norm_gain, head_weight, targets
        )
    N = V * M
    part_cols = block_cols // M
    chunk_cols = width // GATHER_CHUNKS
    slots = V
    any_space = pl.BlockSpec(memory_space=pl.ANY)
    f32, bf16 = jnp.float32, jnp.bfloat16
    dma = pltpu.SemaphoreType.DMA
    result = pl.pallas_call(
        functools.partial(kernel, V, M),
        out_shape=jax.ShapeDtypeStruct((1, LANES), f32),
        in_specs=[pl.BlockSpec(memory_space=pltpu.SMEM)] + [any_space] * 6,
        out_specs=pl.BlockSpec(memory_space=pltpu.VMEM),
        scratch_shapes=[
            pltpu.VMEM((token_rows, width), bf16),
            pltpu.VMEM((token_rows, width), bf16),
            pltpu.VMEM((GATHER_CHUNKS, block_cols, chunk_cols), bf16),
            pltpu.VMEM(residual.shape, bf16),
            pltpu.VMEM((half_width // LANES, LANES), bf16),
            pltpu.VMEM((slots, 1, part_cols), f32),
            pltpu.VMEM((vocab_cols, half_width), bf16),
            pltpu.VMEM((GATHER_CHUNKS, V, token_rows, chunk_cols), bf16),
            pltpu.VMEM((2, T, chunk_cols), f32),
            pltpu.VMEM((N, 1, part_cols), f32),
            pltpu.VMEM((N, 1, part_cols), f32),
            pltpu.VMEM((T, part_cols), f32),
            pltpu.VMEM((T, part_cols), f32),
            pltpu.VMEM((T, part_cols), f32),
            pltpu.VMEM((T, part_cols), bf16),
            pltpu.VMEM((slots, T, part_cols), bf16),
            pltpu.VMEM((N, 1, LANES), f32),
            pltpu.VMEM((M, T // M, vocab_cols), f32),
            pltpu.VMEM((T // M, vocab_cols), f32),
            pltpu.VMEM((V, 1, 3 * LANES), f32),
            dma((5,)),
            dma((GATHER_CHUNKS,)),
            dma((GATHER_CHUNKS, V)),
            dma((GATHER_CHUNKS, V)),
            dma((N,)),
            dma((N,)),
            dma((2,)),
            dma((V,)),
            dma((slots,)),
            dma((N,)),
            dma((N,)),
            dma((2,)),
            dma((V,)),
            dma((V,)),
        ],
        compiler_params=pltpu.CompilerParams(
            collective_id=0, has_side_effects=True, vmem_limit_bytes=56 * 1024 * 1024
        ),
        name="scored_head",
    )(
        targets,
        gate_pre,
        up_pre,
        down_weight,
        residual,
        norm_gain.reshape(-1, LANES),
        head_weight.T,
    )
    return result[0, : targets.shape[0]]


def solution(mesh):
    return jax.shard_map(
        body,
        mesh=mesh,
        in_specs=(
            P(("groups", "vocab"), "mp"),
            P(("groups", "vocab"), "mp"),
            P("vocab", "mp"),
            P(("groups", "vocab", "mp"), None),
            P(),
            P("mp", "vocab"),
            P(("groups", "mp")),
        ),
        out_specs=P(("groups", "mp")),
        check_vma=False,
    )
```

```python
import functools

import jax
import jax.numpy as jnp
from jax import lax
from jax.experimental import pallas as pl
from jax.experimental.pallas import tpu as pltpu
from jax.sharding import PartitionSpec as P

EPSILON = 1e-05


def merged_2(value, axis, combine):
    everything = jax.tree.map(lambda part: lax.all_gather(part, axis), value)
    first = jax.tree.map(lambda part: part[0], everything)

    def turn(k, so_far):
        return combine(so_far, jax.tree.map(lambda part: part[k], everything))

    return lax.fori_loop(1, lax.axis_size(axis), turn, first)


def merge_stats(earlier, follows):
    joint_max = jnp.maximum(earlier[0], follows[0])
    joint_sum = earlier[1] * jnp.exp(earlier[0] - joint_max) + follows[1] * jnp.exp(
        follows[0] - joint_max
    )
    return (joint_max, joint_sum, earlier[2] + follows[2])


def plain_body(gate_pre, up_pre, down_weight, residual, norm_gain, head_weight, targets):
    vocab_count = lax.axis_size("vocab")
    model_count = lax.axis_size("mp")
    model_index = lax.axis_index("mp")
    vocab_index = lax.axis_index("vocab")
    gated_units = (jax.nn.silu(gate_pre.astype(jnp.float32)) * up_pre.astype(jnp.float32)).astype(
        jnp.bfloat16
    )
    down_terms = lax.dot_general(
        lax.all_gather(gated_units, "vocab", axis=0, tiled=True),
        down_weight,
        (((1,), (1,)), ((), ())),
        preferred_element_type=jnp.float32,
    )
    own_rows = residual.shape[0]
    block_cols = down_weight.shape[0]
    grouped = down_terms.reshape(vocab_count, model_count, own_rows, block_cols)
    arrived = lax.all_to_all(
        lax.all_to_all(grouped, "vocab", split_axis=0, concat_axis=3, tiled=True),
        "mp",
        split_axis=1,
        concat_axis=0,
        tiled=True,
    )
    update = jnp.sum(arrived, axis=(0, 1))
    stream = (residual.astype(jnp.float32) + update).astype(jnp.bfloat16)
    stream = lax.optimization_barrier(stream)
    widened = stream.astype(jnp.float32)
    mean_square = jnp.mean(widened * widened, axis=1, keepdims=True)
    normed = (
        widened * lax.rsqrt(mean_square + EPSILON) * norm_gain.astype(jnp.float32)[None, :]
    ).astype(jnp.bfloat16)
    half_width = head_weight.shape[0]
    halves = lax.dynamic_slice_in_dim(
        lax.all_gather(normed, ("vocab", "mp"), axis=0, tiled=True),
        model_index * half_width,
        half_width,
        1,
    )
    logit_terms = jnp.dot(halves, head_weight, preferred_element_type=jnp.float32)
    logits = lax.psum_scatter(logit_terms, "mp", scatter_dimension=0, tiled=True)
    local_ids = targets - vocab_index * logits.shape[1]
    columns = lax.broadcasted_iota(jnp.int32, logits.shape, 1)
    chosen = jnp.sum(jnp.where(columns == local_ids[:, None], logits, 0.0), axis=1)
    row_top = jnp.max(logits, axis=1)
    exp_total = jnp.sum(jnp.exp(logits - row_top[:, None]), axis=1)
    merged = merged_2((row_top, exp_total, chosen), "vocab", merge_stats)
    return merged[2] - merged[0] - jnp.log(merged[1])


GATHER_CHUNKS = 4
MATRIX_SIDE = 256
LANES = 128


def diagonal(rows):
    return lax.broadcasted_iota(jnp.int32, (rows, LANES), 0) == lax.broadcasted_iota(
        jnp.int32, (rows, LANES), 1
    )


def to_lanes(column):
    rows = column.shape[0]
    spread = jnp.where(diagonal(rows), jnp.broadcast_to(column, (rows, LANES)), 0.0)
    return jnp.sum(spread, axis=0, keepdims=True)


def to_rows(lanes, rows):
    spread = jnp.where(diagonal(rows), jnp.broadcast_to(lanes, (rows, LANES)), 0.0)
    return jnp.sum(spread, axis=1, keepdims=True)


def kernel(
    V,
    M,
    targets_ref,
    gate_hbm,
    up_hbm,
    down_hbm,
    residual_hbm,
    gain_hbm,
    head_hbm,
    out_ref,
    gate,
    up,
    down,
    own_residual,
    gain,
    gain_rows,
    head,
    gated_in,
    gated_rows,
    residual_out,
    residual_in,
    residual_rows,
    update_out,
    update_in,
    stream_out,
    stream_in,
    square_in,
    logits_out,
    logits_in,
    stats_in,
    in_sem,
    down_sem,
    gated_send,
    gated_recv,
    residual_send,
    residual_recv,
    update_sem,
    stream_send,
    stream_recv,
    square_send,
    square_recv,
    logits_sem,
    stats_send,
    stats_recv,
):
    v = lax.axis_index("vocab")
    m = lax.axis_index("mp")
    other = 1 - m
    me = v * M + m
    N = V * M
    token_rows, width = gate.shape
    T = V * token_rows
    block_cols = down.shape[1]
    part_cols = block_cols // M
    chunks, _, chunk_cols = down.shape
    own_tokens = T // M
    vocab_cols = head.shape[0]
    half_owner = v // (V // M)

    def peer(i):
        return lax.rem(me + i, N)

    def coords(index):
        return {"vocab": index // M, "mp": lax.rem(index, M)}

    def remote(src, dst, send, recv, vocab, mp):
        return pltpu.make_async_remote_copy(
            src_ref=src,
            dst_ref=dst,
            send_sem=send,
            recv_sem=recv,
            device_id={"vocab": vocab, "mp": mp},
            device_id_type=pl.DeviceIdType.MESH,
        )

    barrier = pltpu.get_barrier_semaphore()
    for i in range(1, N):
        pl.semaphore_signal(
            barrier, inc=1, device_id=coords(peer(i)), device_id_type=pl.DeviceIdType.MESH
        )

    loads = [
        pltpu.make_async_copy(gate_hbm, gate, in_sem.at[0]),
        pltpu.make_async_copy(up_hbm, up, in_sem.at[1]),
        pltpu.make_async_copy(residual_hbm, own_residual, in_sem.at[2]),
        pltpu.make_async_copy(
            gain_hbm.at[pl.ds(pl.multiple_of(m * gain.shape[0], gain.shape[0]), gain.shape[0])],
            gain,
            in_sem.at[3],
        ),
        pltpu.make_async_copy(head_hbm, head, in_sem.at[4]),
    ]
    for load in loads[:3]:
        load.start()

    def down_copy(k):
        return pltpu.make_async_copy(
            down_hbm.at[:, pl.ds(pl.multiple_of(k * chunk_cols, chunk_cols), chunk_cols)],
            down.at[k],
            down_sem.at[k],
        )

    for k in range(chunks):
        down_copy(k).start()
    loads[4].start()
    loads[3].start()

    beside = v + 1 - 2 * lax.rem(v, 2)
    column = V // 2

    def gated_copy(a, source, to, send):
        return remote(
            gated_in.at[a, source],
            gated_in.at[a, source],
            gated_send.at[a, send],
            gated_recv.at[a, source],
            to,
            m,
        )

    def in_column(i):
        return lax.rem(v + 2 * i, V)

    def across(i):
        return lax.rem(beside + 2 * i, V)

    def gated_sends(a):
        return [gated_copy(a, v, in_column(i), i) for i in range(1, column)] + [
            gated_copy(a, v, beside, 0)
        ]

    def gated_relays(a):
        return [gated_copy(a, in_column(i), beside, column + i) for i in range(1, column)]

    def relay_chunk(a):
        for i in range(1, column):
            gated_copy(a, in_column(i), in_column(i), 0).wait_recv()
        for copy in gated_relays(a):
            copy.start()

    def residual_copy(i):
        to = peer(i)
        return remote(
            residual_out.at[to],
            residual_in.at[me],
            residual_send.at[i],
            residual_recv.at[me],
            to // M,
            lax.rem(to, M),
        )

    def residual_arrival(i):
        source = peer(i)
        return remote(
            residual_out.at[source],
            residual_in.at[source],
            residual_send.at[i],
            residual_recv.at[source],
            source // M,
            lax.rem(source, M),
        )

    loads[0].wait()
    loads[1].wait()
    for a in range(chunks):
        part = slice(a * chunk_cols, (a + 1) * chunk_cols)
        g = gate[:, part].astype(jnp.float32)
        u = up[:, part].astype(jnp.float32)
        gated_in[a, v] = (jax.nn.silu(g) * u).astype(jnp.bfloat16)
        if a == 0:
            pl.semaphore_wait(barrier, N - 1)
        for copy in gated_sends(a):
            copy.start()
    loads[2].wait()
    for n in range(N):
        residual_out[n] = own_residual[:, n * part_cols : (n + 1) * part_cols].astype(jnp.float32)
    residual_in[me] = residual_out[me]
    for i in range(1, N):
        residual_copy(i).start()

    def await_chunk(a):
        for i in range(column):
            gated_copy(a, across(i), beside, 0).wait_recv()
        down_copy(a).wait()

    def token_chunk(a):
        for s in range(V):
            gated_rows[a % 2, s * token_rows : (s + 1) * token_rows, :] = gated_in[a, s].astype(
                jnp.float32
            )
        return gated_rows[a % 2].astype(jnp.bfloat16)

    def term(gated, a, which):
        rows = pl.ds(pl.multiple_of(which * part_cols, part_cols), part_cols)
        return lax.dot_general(
            gated,
            down[a, rows, :],
            (((1,), (1,)), ((), ())),
            preferred_element_type=jnp.float32,
        )

    theirs = jnp.zeros((T, part_cols), jnp.float32)
    own = theirs
    relay_chunk(0)
    if chunks > 1:
        relay_chunk(1)
    await_chunk(0)
    gated = token_chunk(0)
    for a in range(chunks):
        theirs = theirs + term(gated, a, other)
        if a == chunks - 1:
            update_out[...] = theirs
            swap = remote(update_out, update_in, update_sem.at[0], update_sem.at[1], v, other)
            swap.start()
            own = own + term(gated, a, m)
        else:
            if a + 2 < chunks:
                relay_chunk(a + 2)
            await_chunk(a + 1)
            following = token_chunk(a + 1)
            own = own + term(gated, a, m)
            gated = following

    loads[3].wait()
    loads[4].wait()
    group = part_cols // LANES
    gains = gain[...].astype(jnp.float32)
    for j in range(V):
        for q in range(group):
            gain_rows[j, :, q * LANES : (q + 1) * LANES] = gains[
                j * group + q : j * group + q + 1
            ]
    for i in range(1, N):
        residual_arrival(i).wait_recv()
    for n in range(N):
        residual_rows[n : n + 1, :] = residual_in[n]
    swap.wait_recv()
    stream = (residual_rows[...] + (own + update_in[...])).astype(jnp.bfloat16)
    stream_out[...] = stream
    wide = stream.astype(jnp.float32)
    square_in[me] = to_lanes(jnp.sum(wide * wide, axis=1, keepdims=True))

    slot = lax.rem(v, V // M) * M + m

    def square_copy(i):
        to = peer(i)
        return remote(
            square_in.at[me],
            square_in.at[me],
            square_send.at[i],
            square_recv.at[me],
            to // M,
            lax.rem(to, M),
        )

    def square_arrival(i):
        source = peer(i)
        return remote(
            square_in.at[source],
            square_in.at[source],
            square_send.at[i],
            square_recv.at[source],
            source // M,
            lax.rem(source, M),
        )

    quarter = V // M

    steps = quarter // 2

    def stream_copy(i, h):
        to = lax.rem(v + 2 * i, quarter) + h * quarter
        return remote(
            stream_out,
            stream_in.at[slot],
            stream_send.at[h * steps + i],
            stream_recv.at[slot],
            to,
            half_owner,
        )

    def over_stream(act):
        for i in range(steps):
            for h in range(M):
                if i:
                    act(stream_copy(i, h))
                else:

                    @pl.when(jnp.logical_or(h != half_owner, m != half_owner))
                    def _():
                        act(stream_copy(i, h))

    def slot_from(base, i, c):
        return lax.rem(lax.rem(base, quarter) + quarter - 2 * i, quarter) * M + c

    def stream_arrival(j):
        return remote(
            stream_out, stream_in.at[j], stream_send.at[0], stream_recv.at[j], v, other
        )

    def stream_relay(i, c):
        j = slot_from(v, i, c)
        return remote(
            stream_in.at[j],
            stream_in.at[j],
            stream_send.at[column + i * M + c],
            stream_recv.at[j],
            beside,
            m,
        )

    for i in range(1, N):
        square_copy(i).start()
    over_stream(lambda copy: copy.start())

    @pl.when(m == half_owner)
    def _():
        stream_in[slot] = stream

    for i in range(steps):
        for c in range(M):
            if i:
                stream_arrival(slot_from(v, i, c)).wait_recv()
            else:

                @pl.when(jnp.logical_or(m != half_owner, m != c))
                def _():
                    stream_arrival(slot_from(v, i, c)).wait_recv()

            stream_relay(i, c).start()

    for i in range(1, N):
        square_arrival(i).wait_recv()
    squares = square_in[0]
    for n in range(1, N):
        squares = squares + square_in[n]
    mean_square = to_rows(squares, T) * (1.0 / (N * part_cols))
    scale = lax.rsqrt(mean_square + EPSILON)

    partial = jnp.zeros((T, vocab_cols), jnp.float32)
    for base in (v, beside):
        for i, c in [(i, c) for i in range(steps) for c in range(M)]:
            j = slot_from(base, i, c)
            if base is beside:
                stream_arrival(j).wait_recv()
            normed = (stream_in[j].astype(jnp.float32) * scale * gain_rows[j]).astype(
                jnp.bfloat16
            )
            features = pl.ds(pl.multiple_of(j * part_cols, part_cols), part_cols)
            partial = partial + lax.dot_general(
                normed,
                head[:, features],
                (((1,), (1,)), ((), ())),
                preferred_element_type=jnp.float32,
            )

    for n in range(M):
        logits_out[n] = partial[n * own_tokens : (n + 1) * own_tokens, :]
    swap_logits = remote(
        logits_out.at[other], logits_in, logits_sem.at[0], logits_sem.at[1], v, other
    )
    swap_logits.start()
    row = lax.broadcasted_iota(jnp.int32, (own_tokens, vocab_cols), 0)
    wanted = jnp.zeros((own_tokens, vocab_cols), jnp.int32)
    for t in range(own_tokens):
        wanted = jnp.where(row == t, targets_ref[t], wanted)
    columns = lax.broadcasted_iota(jnp.int32, (own_tokens, vocab_cols), 1) + v * vocab_cols
    swap_logits.wait_recv()
    logits = logits_out[m] + logits_in[...]
    top = jnp.max(logits, axis=1, keepdims=True)
    total = jnp.sum(jnp.exp(logits - top), axis=1, keepdims=True)
    chosen = jnp.sum(jnp.where(columns == wanted, logits, 0.0), axis=1, keepdims=True)
    stats_in[v, :, 0:LANES] = to_lanes(top)
    stats_in[v, :, LANES : 2 * LANES] = to_lanes(total)
    stats_in[v, :, 2 * LANES : 3 * LANES] = to_lanes(chosen)

    def stats_copy(i):
        return remote(
            stats_in.at[v],
            stats_in.at[v],
            stats_send.at[i],
            stats_recv.at[v],
            lax.rem(v + i, V),
            m,
        )

    def stats_arrival(i):
        source = lax.rem(v + i, V)
        return remote(
            stats_in.at[source],
            stats_in.at[source],
            stats_send.at[i],
            stats_recv.at[source],
            source,
            m,
        )

    for i in range(1, V):
        stats_copy(i).start()
    for a in range(chunks):
        for copy in gated_sends(a) + gated_relays(a):
            copy.wait_send()
    for i in range(1, N):
        residual_copy(i).wait_send()
        square_copy(i).wait_send()
    over_stream(lambda copy: copy.wait_send())
    for i in range(steps):
        for c in range(M):
            stream_relay(i, c).wait_send()

    swap.wait_send()
    swap_logits.wait_send()
    for i in range(1, V):
        stats_arrival(i).wait_recv()
    joint = stats_in[0, :, 0:LANES]
    for n in range(1, V):
        joint = jnp.maximum(joint, stats_in[n, :, 0:LANES])
    exp_total = jnp.zeros((1, LANES), jnp.float32)
    picked = jnp.zeros((1, LANES), jnp.float32)
    for n in range(V):
        exp_total = exp_total + stats_in[n, :, LANES : 2 * LANES] * jnp.exp(
            stats_in[n, :, 0:LANES] - joint
        )
        picked = picked + stats_in[n, :, 2 * LANES : 3 * LANES]
    out_ref[...] = picked - joint - jnp.log(exp_total)
    for i in range(1, V):
        stats_copy(i).wait_send()


def body(gate_pre, up_pre, down_weight, residual, norm_gain, head_weight, targets):
    V = lax.axis_size("vocab")
    M = lax.axis_size("mp")
    token_rows, width = gate_pre.shape
    block_cols = down_weight.shape[0]
    half_width, vocab_cols = head_weight.shape
    T = V * token_rows
    fits = (
        M == 2
        and V % (2 * M) == 0
        and T <= LANES
        and T % 16 == 0
        and residual.shape[0] == 1
        and block_cols % (M * LANES) == 0
        and width % (GATHER_CHUNKS * MATRIX_SIDE) == 0
        and half_width % (16 * LANES) == 0
    )
    if not fits:
        return plain_body(
            gate_pre, up_pre, down_weight, residual, norm_gain, head_weight, targets
        )
    N = V * M
    part_cols = block_cols // M
    chunk_cols = width // GATHER_CHUNKS
    slots = V
    any_space = pl.BlockSpec(memory_space=pl.ANY)
    f32, bf16 = jnp.float32, jnp.bfloat16
    dma = pltpu.SemaphoreType.DMA
    result = pl.pallas_call(
        functools.partial(kernel, V, M),
        out_shape=jax.ShapeDtypeStruct((1, LANES), f32),
        in_specs=[pl.BlockSpec(memory_space=pltpu.SMEM)] + [any_space] * 6,
        out_specs=pl.BlockSpec(memory_space=pltpu.VMEM),
        scratch_shapes=[
            pltpu.VMEM((token_rows, width), bf16),
            pltpu.VMEM((token_rows, width), bf16),
            pltpu.VMEM((GATHER_CHUNKS, block_cols, chunk_cols), bf16),
            pltpu.VMEM(residual.shape, bf16),
            pltpu.VMEM((half_width // LANES, LANES), bf16),
            pltpu.VMEM((slots, 1, part_cols), f32),
            pltpu.VMEM((vocab_cols, half_width), bf16),
            pltpu.VMEM((GATHER_CHUNKS, V, token_rows, chunk_cols), bf16),
            pltpu.VMEM((2, T, chunk_cols), f32),
            pltpu.VMEM((N, 1, part_cols), f32),
            pltpu.VMEM((N, 1, part_cols), f32),
            pltpu.VMEM((T, part_cols), f32),
            pltpu.VMEM((T, part_cols), f32),
            pltpu.VMEM((T, part_cols), f32),
            pltpu.VMEM((T, part_cols), bf16),
            pltpu.VMEM((slots, T, part_cols), bf16),
            pltpu.VMEM((N, 1, LANES), f32),
            pltpu.VMEM((M, T // M, vocab_cols), f32),
            pltpu.VMEM((T // M, vocab_cols), f32),
            pltpu.VMEM((V, 1, 3 * LANES), f32),
            dma((5,)),
            dma((GATHER_CHUNKS,)),
            dma((GATHER_CHUNKS, V)),
            dma((GATHER_CHUNKS, V)),
            dma((N,)),
            dma((N,)),
            dma((2,)),
            dma((V,)),
            dma((slots,)),
            dma((N,)),
            dma((N,)),
            dma((2,)),
            dma((V,)),
            dma((V,)),
        ],
        compiler_params=pltpu.CompilerParams(
            collective_id=0, has_side_effects=True, vmem_limit_bytes=56 * 1024 * 1024
        ),
        name="scored_head",
    )(
        targets,
        gate_pre,
        up_pre,
        down_weight,
        residual,
        norm_gain.reshape(-1, LANES),
        head_weight.T,
    )
    return result[0, : targets.shape[0]]


def solution(mesh):
    return jax.shard_map(
        body,
        mesh=mesh,
        in_specs=(
            P(("groups", "vocab"), "mp"),
            P(("groups", "vocab"), "mp"),
            P("vocab", "mp"),
            P(("groups", "vocab", "mp"), None),
            P(),
            P("mp", "vocab"),
            P(("groups", "mp")),
        ),
        out_specs=P(("groups", "mp")),
        check_vma=False,
    )
```

```python
import functools

import jax
import jax.numpy as jnp
from jax import lax
from jax.experimental import pallas as pl
from jax.experimental.pallas import tpu as pltpu
from jax.sharding import PartitionSpec as P

EPSILON = 1e-05


def merged_2(value, axis, combine):
    everything = jax.tree.map(lambda part: lax.all_gather(part, axis), value)
    first = jax.tree.map(lambda part: part[0], everything)

    def turn(k, so_far):
        return combine(so_far, jax.tree.map(lambda part: part[k], everything))

    return lax.fori_loop(1, lax.axis_size(axis), turn, first)


def merge_stats(earlier, follows):
    joint_max = jnp.maximum(earlier[0], follows[0])
    joint_sum = earlier[1] * jnp.exp(earlier[0] - joint_max) + follows[1] * jnp.exp(
        follows[0] - joint_max
    )
    return (joint_max, joint_sum, earlier[2] + follows[2])


def plain_body(gate_pre, up_pre, down_weight, residual, norm_gain, head_weight, targets):
    vocab_count = lax.axis_size("vocab")
    model_count = lax.axis_size("mp")
    model_index = lax.axis_index("mp")
    vocab_index = lax.axis_index("vocab")
    gated_units = (jax.nn.silu(gate_pre.astype(jnp.float32)) * up_pre.astype(jnp.float32)).astype(
        jnp.bfloat16
    )
    down_terms = lax.dot_general(
        lax.all_gather(gated_units, "vocab", axis=0, tiled=True),
        down_weight,
        (((1,), (1,)), ((), ())),
        preferred_element_type=jnp.float32,
    )
    own_rows = residual.shape[0]
    block_cols = down_weight.shape[0]
    grouped = down_terms.reshape(vocab_count, model_count, own_rows, block_cols)
    arrived = lax.all_to_all(
        lax.all_to_all(grouped, "vocab", split_axis=0, concat_axis=3, tiled=True),
        "mp",
        split_axis=1,
        concat_axis=0,
        tiled=True,
    )
    update = jnp.sum(arrived, axis=(0, 1))
    stream = (residual.astype(jnp.float32) + update).astype(jnp.bfloat16)
    stream = lax.optimization_barrier(stream)
    widened = stream.astype(jnp.float32)
    mean_square = jnp.mean(widened * widened, axis=1, keepdims=True)
    normed = (
        widened * lax.rsqrt(mean_square + EPSILON) * norm_gain.astype(jnp.float32)[None, :]
    ).astype(jnp.bfloat16)
    half_width = head_weight.shape[0]
    halves = lax.dynamic_slice_in_dim(
        lax.all_gather(normed, ("vocab", "mp"), axis=0, tiled=True),
        model_index * half_width,
        half_width,
        1,
    )
    logit_terms = jnp.dot(halves, head_weight, preferred_element_type=jnp.float32)
    logits = lax.psum_scatter(logit_terms, "mp", scatter_dimension=0, tiled=True)
    local_ids = targets - vocab_index * logits.shape[1]
    columns = lax.broadcasted_iota(jnp.int32, logits.shape, 1)
    chosen = jnp.sum(jnp.where(columns == local_ids[:, None], logits, 0.0), axis=1)
    row_top = jnp.max(logits, axis=1)
    exp_total = jnp.sum(jnp.exp(logits - row_top[:, None]), axis=1)
    merged = merged_2((row_top, exp_total, chosen), "vocab", merge_stats)
    return merged[2] - merged[0] - jnp.log(merged[1])


GATHER_CHUNKS = 4
MATRIX_SIDE = 256
LANES = 128


def diagonal(rows):
    return lax.broadcasted_iota(jnp.int32, (rows, LANES), 0) == lax.broadcasted_iota(
        jnp.int32, (rows, LANES), 1
    )


def to_lanes(column):
    rows = column.shape[0]
    spread = jnp.where(diagonal(rows), jnp.broadcast_to(column, (rows, LANES)), 0.0)
    return jnp.sum(spread, axis=0, keepdims=True)


def to_rows(lanes, rows):
    spread = jnp.where(diagonal(rows), jnp.broadcast_to(lanes, (rows, LANES)), 0.0)
    return jnp.sum(spread, axis=1, keepdims=True)


def kernel(
    V,
    M,
    targets_ref,
    gate_hbm,
    up_hbm,
    down_hbm,
    residual_hbm,
    gain_hbm,
    head_hbm,
    out_ref,
    gate,
    up,
    down,
    own_residual,
    gain,
    gain_rows,
    head,
    gated_in,
    gated_rows,
    residual_out,
    residual_in,
    residual_rows,
    update_out,
    update_in,
    stream_out,
    stream_in,
    square_in,
    logits_out,
    logits_in,
    stats_in,
    in_sem,
    down_sem,
    gated_send,
    gated_recv,
    residual_send,
    residual_recv,
    update_sem,
    stream_send,
    stream_recv,
    square_send,
    square_recv,
    logits_sem,
    stats_send,
    stats_recv,
):
    v = lax.axis_index("vocab")
    m = lax.axis_index("mp")
    other = 1 - m
    me = v * M + m
    N = V * M
    token_rows, width = gate.shape
    T = V * token_rows
    block_cols = down.shape[1]
    part_cols = block_cols // M
    chunks, _, chunk_cols = down.shape
    own_tokens = T // M
    vocab_cols = head.shape[0]
    half_owner = v // (V // M)

    def peer(i):
        return lax.rem(me + i, N)

    def coords(index):
        return {"vocab": index // M, "mp": lax.rem(index, M)}

    def remote(src, dst, send, recv, vocab, mp):
        return pltpu.make_async_remote_copy(
            src_ref=src,
            dst_ref=dst,
            send_sem=send,
            recv_sem=recv,
            device_id={"vocab": vocab, "mp": mp},
            device_id_type=pl.DeviceIdType.MESH,
        )

    barrier = pltpu.get_barrier_semaphore()
    for i in range(1, N):
        pl.semaphore_signal(
            barrier, inc=1, device_id=coords(peer(i)), device_id_type=pl.DeviceIdType.MESH
        )

    loads = [
        pltpu.make_async_copy(gate_hbm, gate, in_sem.at[0]),
        pltpu.make_async_copy(up_hbm, up, in_sem.at[1]),
        pltpu.make_async_copy(residual_hbm, own_residual, in_sem.at[2]),
        pltpu.make_async_copy(
            gain_hbm.at[pl.ds(pl.multiple_of(m * gain.shape[0], gain.shape[0]), gain.shape[0])],
            gain,
            in_sem.at[3],
        ),
        pltpu.make_async_copy(head_hbm, head, in_sem.at[4]),
    ]
    for load in loads[:3]:
        load.start()

    pieces = down_sem.shape[1]
    piece_rows = block_cols // pieces

    def down_copies(k):
        return [
            pltpu.make_async_copy(
                down_hbm.at[
                    p * piece_rows : (p + 1) * piece_rows,
                    k * chunk_cols : (k + 1) * chunk_cols,
                ],
                down.at[k, p * piece_rows : (p + 1) * piece_rows],
                down_sem.at[k, p],
            )
            for p in range(pieces)
        ]

    for k in range(chunks):
        for copy in down_copies(k):
            copy.start()
    loads[4].start()
    loads[3].start()

    def gated_copy(a, i):
        to = lax.rem(v + i, V)
        return remote(
            gated_in.at[a, v], gated_in.at[a, v], gated_send.at[a, i], gated_recv.at[a, v], to, m
        )

    def gated_arrival(a, i):
        source = lax.rem(v + i, V)
        return remote(
            gated_in.at[a, source],
            gated_in.at[a, source],
            gated_send.at[a, i],
            gated_recv.at[a, source],
            source,
            m,
        )

    def residual_copy(i):
        to = peer(i)
        return remote(
            residual_out.at[to],
            residual_in.at[me],
            residual_send.at[i],
            residual_recv.at[me],
            to // M,
            lax.rem(to, M),
        )

    def residual_arrival(i):
        source = peer(i)
        return remote(
            residual_out.at[source],
            residual_in.at[source],
            residual_send.at[i],
            residual_recv.at[source],
            source // M,
            lax.rem(source, M),
        )

    loads[0].wait()
    loads[1].wait()
    for a in range(chunks):
        part = slice(a * chunk_cols, (a + 1) * chunk_cols)
        g = gate[:, part].astype(jnp.float32)
        u = up[:, part].astype(jnp.float32)
        gated_in[a, v] = (jax.nn.silu(g) * u).astype(jnp.bfloat16)
        if a == 0:
            pl.semaphore_wait(barrier, N - 1)
        for i in range(1, V):
            gated_copy(a, i).start()
    loads[2].wait()
    for n in range(N):
        residual_out[n] = own_residual[:, n * part_cols : (n + 1) * part_cols].astype(jnp.float32)
    residual_in[me] = residual_out[me]
    for i in range(1, N):
        residual_copy(i).start()

    def await_chunk(a):
        for i in range(1, V):
            gated_arrival(a, i).wait_recv()
        for copy in down_copies(a):
            copy.wait()

    def token_chunk(a):
        for s in range(V):
            gated_rows[a % 2, s * token_rows : (s + 1) * token_rows, :] = gated_in[a, s].astype(
                jnp.float32
            )
        return gated_rows[a % 2].astype(jnp.bfloat16)

    def contract(left, right):
        return lax.dot_general(
            left, right, (((1,), (1,)), ((), ())), preferred_element_type=jnp.float32
        )

    def block(a, which, part):
        rows = pl.ds(pl.multiple_of(which * part_cols, part_cols), part_cols)
        return down[a, rows, part]

    theirs = jnp.zeros((T, part_cols), jnp.float32)
    own = jnp.zeros((part_cols, T), jnp.float32)
    parts = [slice(k, k + MATRIX_SIDE) for k in range(0, chunk_cols, MATRIX_SIDE)]
    for a in range(chunks):
        await_chunk(a)
        gated = token_chunk(a)
        if a < chunks - 1:
            for part in parts:
                theirs = theirs + contract(gated[:, part], block(a, other, part))
                own = own + contract(block(a, m, part), gated[:, part])
        else:
            update_out[...] = theirs + contract(gated, block(a, other, slice(0, chunk_cols)))
            swap = remote(update_out, update_in, update_sem.at[0], update_sem.at[1], v, other)
            swap.start()
            own = own + contract(block(a, m, slice(0, chunk_cols)), gated)

    loads[3].wait()
    loads[4].wait()
    group = part_cols // LANES
    gains = gain[...].astype(jnp.float32)
    for j in range(V):
        for q in range(group):
            gain_rows[j, :, q * LANES : (q + 1) * LANES] = gains[
                j * group + q : j * group + q + 1
            ]
    for i in range(1, N):
        residual_arrival(i).wait_recv()
    for n in range(N):
        residual_rows[n : n + 1, :] = residual_in[n]
    swap.wait_recv()
    stream = (residual_rows[...] + (own.T + update_in[...])).astype(jnp.bfloat16)
    stream_out[...] = stream
    wide = stream.astype(jnp.float32)
    square_in[me] = to_lanes(jnp.sum(wide * wide, axis=1, keepdims=True))

    slot = lax.rem(v, V // M) * M + m

    def square_copy(i):
        to = peer(i)
        return remote(
            square_in.at[me],
            square_in.at[me],
            square_send.at[i],
            square_recv.at[me],
            to // M,
            lax.rem(to, M),
        )

    def square_arrival(i):
        source = peer(i)
        return remote(
            square_in.at[source],
            square_in.at[source],
            square_send.at[i],
            square_recv.at[source],
            source // M,
            lax.rem(source, M),
        )

    quarter = V // M

    def stream_copy(i, h):
        to = lax.rem(v + i, quarter) + h * quarter
        return remote(
            stream_out,
            stream_in.at[slot],
            stream_send.at[h * quarter + i],
            stream_recv.at[slot],
            to,
            half_owner,
        )

    def over_stream(act):
        for i in range(quarter):
            for h in range(M):
                if i:
                    act(stream_copy(i, h))
                else:

                    @pl.when(jnp.logical_or(h != half_owner, m != half_owner))
                    def _():
                        act(stream_copy(i, h))

    def stream_arrival(j):
        return remote(
            stream_out, stream_in.at[j], stream_send.at[0], stream_recv.at[j], v, other
        )

    for i in range(1, N):
        square_copy(i).start()
    over_stream(lambda copy: copy.start())

    @pl.when(m == half_owner)
    def _():
        stream_in[slot] = stream

    for i in range(1, N):
        square_arrival(i).wait_recv()
    squares = square_in[0]
    for n in range(1, N):
        squares = squares + square_in[n]
    mean_square = to_rows(squares, T) * (1.0 / (N * part_cols))
    scale = lax.rsqrt(mean_square + EPSILON)

    partial = jnp.zeros((T, vocab_cols), jnp.float32)
    for i in range(quarter):
        source = lax.rem(v + quarter - i, quarter)
        for c in range(M):
            j = source * M + c
            if i:
                stream_arrival(j).wait_recv()
            else:

                @pl.when(jnp.logical_or(m != half_owner, m != c))
                def _():
                    stream_arrival(j).wait_recv()

            normed = (stream_in[j].astype(jnp.float32) * scale * gain_rows[j]).astype(
                jnp.bfloat16
            )
            features = pl.ds(pl.multiple_of(j * part_cols, part_cols), part_cols)
            partial = partial + lax.dot_general(
                normed,
                head[:, features],
                (((1,), (1,)), ((), ())),
                preferred_element_type=jnp.float32,
            )

    for n in range(M):
        logits_out[n] = partial[n * own_tokens : (n + 1) * own_tokens, :]
    swap_logits = remote(
        logits_out.at[other], logits_in, logits_sem.at[0], logits_sem.at[1], v, other
    )
    swap_logits.start()
    row = lax.broadcasted_iota(jnp.int32, (own_tokens, vocab_cols), 0)
    wanted = jnp.zeros((own_tokens, vocab_cols), jnp.int32)
    for t in range(own_tokens):
        wanted = jnp.where(row == t, targets_ref[t], wanted)
    columns = lax.broadcasted_iota(jnp.int32, (own_tokens, vocab_cols), 1) + v * vocab_cols
    swap_logits.wait_recv()
    logits = logits_out[m] + logits_in[...]
    top = jnp.max(logits, axis=1, keepdims=True)
    total = jnp.sum(jnp.exp(logits - top), axis=1, keepdims=True)
    chosen = jnp.sum(jnp.where(columns == wanted, logits, 0.0), axis=1, keepdims=True)
    stats_in[v, :, 0:LANES] = to_lanes(top)
    stats_in[v, :, LANES : 2 * LANES] = to_lanes(total)
    stats_in[v, :, 2 * LANES : 3 * LANES] = to_lanes(chosen)

    def stats_copy(i):
        return remote(
            stats_in.at[v],
            stats_in.at[v],
            stats_send.at[i],
            stats_recv.at[v],
            lax.rem(v + i, V),
            m,
        )

    def stats_arrival(i):
        source = lax.rem(v + i, V)
        return remote(
            stats_in.at[source],
            stats_in.at[source],
            stats_send.at[i],
            stats_recv.at[source],
            source,
            m,
        )

    for i in range(1, V):
        stats_copy(i).start()
    for a in range(chunks):
        for i in range(1, V):
            gated_copy(a, i).wait_send()
    for i in range(1, N):
        residual_copy(i).wait_send()
        square_copy(i).wait_send()
    over_stream(lambda copy: copy.wait_send())

    swap.wait_send()
    swap_logits.wait_send()
    for i in range(1, V):
        stats_arrival(i).wait_recv()
    joint = stats_in[0, :, 0:LANES]
    for n in range(1, V):
        joint = jnp.maximum(joint, stats_in[n, :, 0:LANES])
    exp_total = jnp.zeros((1, LANES), jnp.float32)
    picked = jnp.zeros((1, LANES), jnp.float32)
    for n in range(V):
        exp_total = exp_total + stats_in[n, :, LANES : 2 * LANES] * jnp.exp(
            stats_in[n, :, 0:LANES] - joint
        )
        picked = picked + stats_in[n, :, 2 * LANES : 3 * LANES]
    out_ref[...] = picked - joint - jnp.log(exp_total)
    for i in range(1, V):
        stats_copy(i).wait_send()


def body(gate_pre, up_pre, down_weight, residual, norm_gain, head_weight, targets):
    V = lax.axis_size("vocab")
    M = lax.axis_size("mp")
    token_rows, width = gate_pre.shape
    block_cols = down_weight.shape[0]
    half_width, vocab_cols = head_weight.shape
    T = V * token_rows
    fits = (
        M == 2
        and V % M == 0
        and T <= LANES
        and T % 16 == 0
        and residual.shape[0] == 1
        and block_cols % (M * LANES) == 0
        and block_cols % 64 == 0
        and width % (GATHER_CHUNKS * MATRIX_SIDE) == 0
        and half_width % (16 * LANES) == 0
    )
    if not fits:
        return plain_body(
            gate_pre, up_pre, down_weight, residual, norm_gain, head_weight, targets
        )
    N = V * M
    part_cols = block_cols // M
    chunk_cols = width // GATHER_CHUNKS
    slots = V
    any_space = pl.BlockSpec(memory_space=pl.ANY)
    f32, bf16 = jnp.float32, jnp.bfloat16
    dma = pltpu.SemaphoreType.DMA
    result = pl.pallas_call(
        functools.partial(kernel, V, M),
        out_shape=jax.ShapeDtypeStruct((1, LANES), f32),
        in_specs=[pl.BlockSpec(memory_space=pltpu.SMEM)] + [any_space] * 6,
        out_specs=pl.BlockSpec(memory_space=pltpu.VMEM),
        scratch_shapes=[
            pltpu.VMEM((token_rows, width), bf16),
            pltpu.VMEM((token_rows, width), bf16),
            pltpu.VMEM((GATHER_CHUNKS, block_cols, chunk_cols), bf16),
            pltpu.VMEM(residual.shape, bf16),
            pltpu.VMEM((half_width // LANES, LANES), bf16),
            pltpu.VMEM((slots, 1, part_cols), f32),
            pltpu.VMEM((vocab_cols, half_width), bf16),
            pltpu.VMEM((GATHER_CHUNKS, V, token_rows, chunk_cols), bf16),
            pltpu.VMEM((2, T, chunk_cols), f32),
            pltpu.VMEM((N, 1, part_cols), f32),
            pltpu.VMEM((N, 1, part_cols), f32),
            pltpu.VMEM((T, part_cols), f32),
            pltpu.VMEM((T, part_cols), f32),
            pltpu.VMEM((T, part_cols), f32),
            pltpu.VMEM((T, part_cols), bf16),
            pltpu.VMEM((slots, T, part_cols), bf16),
            pltpu.VMEM((N, 1, LANES), f32),
            pltpu.VMEM((M, T // M, vocab_cols), f32),
            pltpu.VMEM((T // M, vocab_cols), f32),
            pltpu.VMEM((V, 1, 3 * LANES), f32),
            dma((5,)),
            dma((GATHER_CHUNKS, 4)),
            dma((GATHER_CHUNKS, V)),
            dma((GATHER_CHUNKS, V)),
            dma((N,)),
            dma((N,)),
            dma((2,)),
            dma((V,)),
            dma((slots,)),
            dma((N,)),
            dma((N,)),
            dma((2,)),
            dma((V,)),
            dma((V,)),
        ],
        compiler_params=pltpu.CompilerParams(
            collective_id=0, has_side_effects=True, vmem_limit_bytes=56 * 1024 * 1024
        ),
        name="scored_head",
    )(
        targets,
        gate_pre,
        up_pre,
        down_weight,
        residual,
        norm_gain.reshape(-1, LANES),
        head_weight.T,
    )
    return result[0, : targets.shape[0]]


def solution(mesh):
    return jax.shard_map(
        body,
        mesh=mesh,
        in_specs=(
            P(("groups", "vocab"), "mp"),
            P(("groups", "vocab"), "mp"),
            P("vocab", "mp"),
            P(("groups", "vocab", "mp"), None),
            P(),
            P("mp", "vocab"),
            P(("groups", "mp")),
        ),
        out_specs=P(("groups", "mp")),
        check_vma=False,
    )
```

```python
import functools

import jax
import jax.numpy as jnp
from jax import lax
from jax.experimental import pallas as pl
from jax.experimental.pallas import tpu as pltpu
from jax.sharding import PartitionSpec as P

EPSILON = 1e-05


def merged_2(value, axis, combine):
    everything = jax.tree.map(lambda part: lax.all_gather(part, axis), value)
    first = jax.tree.map(lambda part: part[0], everything)

    def turn(k, so_far):
        return combine(so_far, jax.tree.map(lambda part: part[k], everything))

    return lax.fori_loop(1, lax.axis_size(axis), turn, first)


def merge_stats(earlier, follows):
    joint_max = jnp.maximum(earlier[0], follows[0])
    joint_sum = earlier[1] * jnp.exp(earlier[0] - joint_max) + follows[1] * jnp.exp(
        follows[0] - joint_max
    )
    return (joint_max, joint_sum, earlier[2] + follows[2])


def plain_body(gate_pre, up_pre, down_weight, residual, norm_gain, head_weight, targets):
    vocab_count = lax.axis_size("vocab")
    model_count = lax.axis_size("mp")
    model_index = lax.axis_index("mp")
    vocab_index = lax.axis_index("vocab")
    gated_units = (jax.nn.silu(gate_pre.astype(jnp.float32)) * up_pre.astype(jnp.float32)).astype(
        jnp.bfloat16
    )
    down_terms = lax.dot_general(
        lax.all_gather(gated_units, "vocab", axis=0, tiled=True),
        down_weight,
        (((1,), (1,)), ((), ())),
        preferred_element_type=jnp.float32,
    )
    own_rows = residual.shape[0]
    block_cols = down_weight.shape[0]
    grouped = down_terms.reshape(vocab_count, model_count, own_rows, block_cols)
    arrived = lax.all_to_all(
        lax.all_to_all(grouped, "vocab", split_axis=0, concat_axis=3, tiled=True),
        "mp",
        split_axis=1,
        concat_axis=0,
        tiled=True,
    )
    update = jnp.sum(arrived, axis=(0, 1))
    stream = (residual.astype(jnp.float32) + update).astype(jnp.bfloat16)
    stream = lax.optimization_barrier(stream)
    widened = stream.astype(jnp.float32)
    mean_square = jnp.mean(widened * widened, axis=1, keepdims=True)
    normed = (
        widened * lax.rsqrt(mean_square + EPSILON) * norm_gain.astype(jnp.float32)[None, :]
    ).astype(jnp.bfloat16)
    half_width = head_weight.shape[0]
    halves = lax.dynamic_slice_in_dim(
        lax.all_gather(normed, ("vocab", "mp"), axis=0, tiled=True),
        model_index * half_width,
        half_width,
        1,
    )
    logit_terms = jnp.dot(halves, head_weight, preferred_element_type=jnp.float32)
    logits = lax.psum_scatter(logit_terms, "mp", scatter_dimension=0, tiled=True)
    local_ids = targets - vocab_index * logits.shape[1]
    columns = lax.broadcasted_iota(jnp.int32, logits.shape, 1)
    chosen = jnp.sum(jnp.where(columns == local_ids[:, None], logits, 0.0), axis=1)
    row_top = jnp.max(logits, axis=1)
    exp_total = jnp.sum(jnp.exp(logits - row_top[:, None]), axis=1)
    merged = merged_2((row_top, exp_total, chosen), "vocab", merge_stats)
    return merged[2] - merged[0] - jnp.log(merged[1])


GATHER_CHUNKS = 4
MATRIX_SIDE = 256
LANES = 128


def diagonal(rows):
    return lax.broadcasted_iota(jnp.int32, (rows, LANES), 0) == lax.broadcasted_iota(
        jnp.int32, (rows, LANES), 1
    )


def to_lanes(column):
    rows = column.shape[0]
    spread = jnp.where(diagonal(rows), jnp.broadcast_to(column, (rows, LANES)), 0.0)
    return jnp.sum(spread, axis=0, keepdims=True)


def to_rows(lanes, rows):
    spread = jnp.where(diagonal(rows), jnp.broadcast_to(lanes, (rows, LANES)), 0.0)
    return jnp.sum(spread, axis=1, keepdims=True)


def kernel(
    V,
    M,
    targets_ref,
    gate_hbm,
    up_hbm,
    down_hbm,
    residual_hbm,
    gain_hbm,
    head_hbm,
    out_ref,
    gate,
    up,
    down,
    own_residual,
    gain,
    gain_rows,
    head,
    gated_in,
    gated_rows,
    residual_out,
    residual_in,
    residual_rows,
    update_out,
    update_in,
    stream_out,
    stream_in,
    square_in,
    logits_out,
    logits_in,
    stats_in,
    in_sem,
    down_sem,
    head_sem,
    gated_send,
    gated_recv,
    residual_send,
    residual_recv,
    update_sem,
    stream_send,
    stream_recv,
    square_send,
    square_recv,
    logits_sem,
    stats_send,
    stats_recv,
):
    v = lax.axis_index("vocab")
    m = lax.axis_index("mp")
    other = 1 - m
    me = v * M + m
    N = V * M
    token_rows, width = gate.shape
    T = V * token_rows
    chunks, tiles, block_cols, _ = down.shape
    part_cols = block_cols // M
    chunk_cols = tiles * LANES
    own_tokens = T // M
    vocab_cols = head.shape[1]
    half_owner = v // (V // M)

    def peer(i):
        return lax.rem(me + i, N)

    def coords(index):
        return {"vocab": index // M, "mp": lax.rem(index, M)}

    def remote(src, dst, send, recv, vocab, mp):
        return pltpu.make_async_remote_copy(
            src_ref=src,
            dst_ref=dst,
            send_sem=send,
            recv_sem=recv,
            device_id={"vocab": vocab, "mp": mp},
            device_id_type=pl.DeviceIdType.MESH,
        )

    barrier = pltpu.get_barrier_semaphore()
    for i in range(1, N):
        pl.semaphore_signal(
            barrier, inc=1, device_id=coords(peer(i)), device_id_type=pl.DeviceIdType.MESH
        )

    loads = [
        pltpu.make_async_copy(gate_hbm, gate, in_sem.at[0]),
        pltpu.make_async_copy(up_hbm, up, in_sem.at[1]),
        pltpu.make_async_copy(residual_hbm, own_residual, in_sem.at[2]),
        pltpu.make_async_copy(
            gain_hbm.at[pl.ds(pl.multiple_of(m * gain.shape[0], gain.shape[0]), gain.shape[0])],
            gain,
            in_sem.at[3],
        ),
    ]
    for load in loads[:3]:
        load.start()

    def down_copy(k, t):
        first = pl.multiple_of((k * tiles + t) * LANES, LANES)
        return pltpu.make_async_copy(
            down_hbm.at[:, pl.ds(first, LANES)], down.at[k, t], down_sem.at[k, t]
        )

    def head_copy(t):
        first = pl.multiple_of(t * LANES, LANES)
        return pltpu.make_async_copy(
            head_hbm.at[:, pl.ds(first, LANES)], head.at[t], head_sem.at[t]
        )

    def start_weights(k):
        @pl.loop(0, tiles)
        def _(t):
            down_copy(k, t).start()

    early = min(2, chunks)
    for k in range(early):
        start_weights(k)
    loads[3].start()

    def gated_copy(a, i):
        to = lax.rem(v + i, V)
        return remote(
            gated_in.at[a, v], gated_in.at[a, v], gated_send.at[a, i], gated_recv.at[a, v], to, m
        )

    def gated_arrival(a, i):
        source = lax.rem(v + i, V)
        return remote(
            gated_in.at[a, source],
            gated_in.at[a, source],
            gated_send.at[a, i],
            gated_recv.at[a, source],
            source,
            m,
        )

    def residual_copy(i):
        to = peer(i)
        return remote(
            residual_out.at[to],
            residual_in.at[me],
            residual_send.at[i],
            residual_recv.at[me],
            to // M,
            lax.rem(to, M),
        )

    def residual_arrival(i):
        source = peer(i)
        return remote(
            residual_out.at[source],
            residual_in.at[source],
            residual_send.at[i],
            residual_recv.at[source],
            source // M,
            lax.rem(source, M),
        )

    loads[0].wait()
    loads[1].wait()
    for a in range(chunks):
        part = slice(a * chunk_cols, (a + 1) * chunk_cols)
        g = gate[:, part].astype(jnp.float32)
        u = up[:, part].astype(jnp.float32)
        gated_in[a, v] = (jax.nn.silu(g) * u).astype(jnp.bfloat16)
        if a == 0:
            pl.semaphore_wait(barrier, N - 1)
        for i in range(1, V):
            gated_copy(a, i).start()
    for k in range(early, chunks):
        start_weights(k)

    @pl.loop(0, head.shape[0])
    def _(t):
        head_copy(t).start()

    loads[2].wait()
    for n in range(N):
        residual_out[n] = own_residual[:, n * part_cols : (n + 1) * part_cols].astype(jnp.float32)
    residual_in[me] = residual_out[me]
    for i in range(1, N):
        residual_copy(i).start()

    def await_chunk(a):
        for i in range(1, V):
            gated_arrival(a, i).wait_recv()

        @pl.loop(0, tiles)
        def _(t):
            down_copy(a, t).wait()

    def token_chunk(a):
        for s in range(V):
            gated_rows[a % 2, s * token_rows : (s + 1) * token_rows, :] = gated_in[a, s].astype(
                jnp.float32
            )
        return gated_rows[a % 2].astype(jnp.bfloat16)

    def term(gated, a, which):
        rows = pl.ds(pl.multiple_of(which * part_cols, part_cols), part_cols)
        return lax.dot_general(
            gated,
            jnp.concatenate([down[a, t, rows, :] for t in range(tiles)], axis=1),
            (((1,), (1,)), ((), ())),
            preferred_element_type=jnp.float32,
        )

    theirs = jnp.zeros((T, part_cols), jnp.float32)
    own = theirs
    await_chunk(0)
    gated = token_chunk(0)
    for a in range(chunks):
        theirs = theirs + term(gated, a, other)
        if a == chunks - 1:
            update_out[...] = theirs
            swap = remote(update_out, update_in, update_sem.at[0], update_sem.at[1], v, other)
            swap.start()
            own = own + term(gated, a, m)
        else:
            await_chunk(a + 1)
            following = token_chunk(a + 1)
            own = own + term(gated, a, m)
            gated = following

    loads[3].wait()

    @pl.loop(0, head.shape[0])
    def _(t):
        head_copy(t).wait()

    group = part_cols // LANES
    gains = gain[...].astype(jnp.float32)
    for j in range(V):
        for q in range(group):
            gain_rows[j, :, q * LANES : (q + 1) * LANES] = gains[
                j * group + q : j * group + q + 1
            ]
    for i in range(1, N):
        residual_arrival(i).wait_recv()
    for n in range(N):
        residual_rows[n : n + 1, :] = residual_in[n]
    swap.wait_recv()
    stream = (residual_rows[...] + (own + update_in[...])).astype(jnp.bfloat16)
    stream_out[...] = stream
    wide = stream.astype(jnp.float32)
    square_in[me] = to_lanes(jnp.sum(wide * wide, axis=1, keepdims=True))

    slot = lax.rem(v, V // M) * M + m

    def square_copy(i):
        to = peer(i)
        return remote(
            square_in.at[me],
            square_in.at[me],
            square_send.at[i],
            square_recv.at[me],
            to // M,
            lax.rem(to, M),
        )

    def square_arrival(i):
        source = peer(i)
        return remote(
            square_in.at[source],
            square_in.at[source],
            square_send.at[i],
            square_recv.at[source],
            source // M,
            lax.rem(source, M),
        )

    quarter = V // M

    def stream_copy(i, h):
        to = lax.rem(v + i, quarter) + h * quarter
        return remote(
            stream_out,
            stream_in.at[slot],
            stream_send.at[h * quarter + i],
            stream_recv.at[slot],
            to,
            half_owner,
        )

    def over_stream(act):
        for i in range(quarter):
            for h in range(M):
                if i:
                    act(stream_copy(i, h))
                else:

                    @pl.when(jnp.logical_or(h != half_owner, m != half_owner))
                    def _():
                        act(stream_copy(i, h))

    def stream_arrival(j):
        return remote(
            stream_out, stream_in.at[j], stream_send.at[0], stream_recv.at[j], v, other
        )

    for i in range(1, N):
        square_copy(i).start()
    over_stream(lambda copy: copy.start())

    @pl.when(m == half_owner)
    def _():
        stream_in[slot] = stream

    for i in range(1, N):
        square_arrival(i).wait_recv()
    squares = square_in[0]
    for n in range(1, N):
        squares = squares + square_in[n]
    mean_square = to_rows(squares, T) * (1.0 / (N * part_cols))
    scale = lax.rsqrt(mean_square + EPSILON)

    partial = jnp.zeros((T, vocab_cols), jnp.float32)
    for i in range(quarter):
        source = lax.rem(v + quarter - i, quarter)
        for c in range(M):
            j = source * M + c
            if i:
                stream_arrival(j).wait_recv()
            else:

                @pl.when(jnp.logical_or(m != half_owner, m != c))
                def _():
                    stream_arrival(j).wait_recv()

            normed = (stream_in[j].astype(jnp.float32) * scale * gain_rows[j]).astype(
                jnp.bfloat16
            )
            partial = partial + lax.dot_general(
                normed,
                jnp.concatenate([head[j * group + q] for q in range(group)], axis=1),
                (((1,), (1,)), ((), ())),
                preferred_element_type=jnp.float32,
            )

    for n in range(M):
        logits_out[n] = partial[n * own_tokens : (n + 1) * own_tokens, :]
    swap_logits = remote(
        logits_out.at[other], logits_in, logits_sem.at[0], logits_sem.at[1], v, other
    )
    swap_logits.start()
    row = lax.broadcasted_iota(jnp.int32, (own_tokens, vocab_cols), 0)
    wanted = jnp.zeros((own_tokens, vocab_cols), jnp.int32)
    for t in range(own_tokens):
        wanted = jnp.where(row == t, targets_ref[t], wanted)
    columns = lax.broadcasted_iota(jnp.int32, (own_tokens, vocab_cols), 1) + v * vocab_cols
    swap_logits.wait_recv()
    logits = logits_out[m] + logits_in[...]
    top = jnp.max(logits, axis=1, keepdims=True)
    total = jnp.sum(jnp.exp(logits - top), axis=1, keepdims=True)
    chosen = jnp.sum(jnp.where(columns == wanted, logits, 0.0), axis=1, keepdims=True)
    stats_in[v, :, 0:LANES] = to_lanes(top)
    stats_in[v, :, LANES : 2 * LANES] = to_lanes(total)
    stats_in[v, :, 2 * LANES : 3 * LANES] = to_lanes(chosen)

    def stats_copy(i):
        return remote(
            stats_in.at[v],
            stats_in.at[v],
            stats_send.at[i],
            stats_recv.at[v],
            lax.rem(v + i, V),
            m,
        )

    def stats_arrival(i):
        source = lax.rem(v + i, V)
        return remote(
            stats_in.at[source],
            stats_in.at[source],
            stats_send.at[i],
            stats_recv.at[source],
            source,
            m,
        )

    for i in range(1, V):
        stats_copy(i).start()
    for a in range(chunks):
        for i in range(1, V):
            gated_copy(a, i).wait_send()
    for i in range(1, N):
        residual_copy(i).wait_send()
        square_copy(i).wait_send()
    over_stream(lambda copy: copy.wait_send())

    swap.wait_send()
    swap_logits.wait_send()
    for i in range(1, V):
        stats_arrival(i).wait_recv()
    joint = stats_in[0, :, 0:LANES]
    for n in range(1, V):
        joint = jnp.maximum(joint, stats_in[n, :, 0:LANES])
    exp_total = jnp.zeros((1, LANES), jnp.float32)
    picked = jnp.zeros((1, LANES), jnp.float32)
    for n in range(V):
        exp_total = exp_total + stats_in[n, :, LANES : 2 * LANES] * jnp.exp(
            stats_in[n, :, 0:LANES] - joint
        )
        picked = picked + stats_in[n, :, 2 * LANES : 3 * LANES]
    out_ref[...] = picked - joint - jnp.log(exp_total)
    for i in range(1, V):
        stats_copy(i).wait_send()


def body(gate_pre, up_pre, down_weight, residual, norm_gain, head_weight, targets):
    V = lax.axis_size("vocab")
    M = lax.axis_size("mp")
    token_rows, width = gate_pre.shape
    block_cols = down_weight.shape[0]
    half_width, vocab_cols = head_weight.shape
    T = V * token_rows
    fits = (
        M == 2
        and V % M == 0
        and T <= LANES
        and T % 16 == 0
        and residual.shape[0] == 1
        and block_cols % (M * LANES) == 0
        and width % (GATHER_CHUNKS * MATRIX_SIDE) == 0
        and half_width % (16 * LANES) == 0
    )
    if not fits:
        return plain_body(
            gate_pre, up_pre, down_weight, residual, norm_gain, head_weight, targets
        )
    N = V * M
    part_cols = block_cols // M
    chunk_cols = width // GATHER_CHUNKS
    slots = V
    any_space = pl.BlockSpec(memory_space=pl.ANY)
    f32, bf16 = jnp.float32, jnp.bfloat16
    dma = pltpu.SemaphoreType.DMA
    result = pl.pallas_call(
        functools.partial(kernel, V, M),
        out_shape=jax.ShapeDtypeStruct((1, LANES), f32),
        in_specs=[pl.BlockSpec(memory_space=pltpu.SMEM)] + [any_space] * 6,
        out_specs=pl.BlockSpec(memory_space=pltpu.VMEM),
        scratch_shapes=[
            pltpu.VMEM((token_rows, width), bf16),
            pltpu.VMEM((token_rows, width), bf16),
            pltpu.VMEM((GATHER_CHUNKS, chunk_cols // LANES, block_cols, LANES), bf16),
            pltpu.VMEM(residual.shape, bf16),
            pltpu.VMEM((half_width // LANES, LANES), bf16),
            pltpu.VMEM((slots, 1, part_cols), f32),
            pltpu.VMEM((half_width // LANES, vocab_cols, LANES), bf16),
            pltpu.VMEM((GATHER_CHUNKS, V, token_rows, chunk_cols), bf16),
            pltpu.VMEM((2, T, chunk_cols), f32),
            pltpu.VMEM((N, 1, part_cols), f32),
            pltpu.VMEM((N, 1, part_cols), f32),
            pltpu.VMEM((T, part_cols), f32),
            pltpu.VMEM((T, part_cols), f32),
            pltpu.VMEM((T, part_cols), f32),
            pltpu.VMEM((T, part_cols), bf16),
            pltpu.VMEM((slots, T, part_cols), bf16),
            pltpu.VMEM((N, 1, LANES), f32),
            pltpu.VMEM((M, T // M, vocab_cols), f32),
            pltpu.VMEM((T // M, vocab_cols), f32),
            pltpu.VMEM((V, 1, 3 * LANES), f32),
            dma((4,)),
            dma((GATHER_CHUNKS, chunk_cols // LANES)),
            dma((half_width // LANES,)),
            dma((GATHER_CHUNKS, V)),
            dma((GATHER_CHUNKS, V)),
            dma((N,)),
            dma((N,)),
            dma((2,)),
            dma((V,)),
            dma((slots,)),
            dma((N,)),
            dma((N,)),
            dma((2,)),
            dma((V,)),
            dma((V,)),
        ],
        compiler_params=pltpu.CompilerParams(
            collective_id=0, has_side_effects=True, vmem_limit_bytes=56 * 1024 * 1024
        ),
        name="scored_head",
    )(
        targets,
        gate_pre,
        up_pre,
        down_weight,
        residual,
        norm_gain.reshape(-1, LANES),
        head_weight.T,
    )
    return result[0, : targets.shape[0]]


def solution(mesh):
    return jax.shard_map(
        body,
        mesh=mesh,
        in_specs=(
            P(("groups", "vocab"), "mp"),
            P(("groups", "vocab"), "mp"),
            P("vocab", "mp"),
            P(("groups", "vocab", "mp"), None),
            P(),
            P("mp", "vocab"),
            P(("groups", "mp")),
        ),
        out_specs=P(("groups", "mp")),
        check_vma=False,
    )
```

```python
import functools

import jax
import jax.numpy as jnp
from jax import lax
from jax.experimental import pallas as pl
from jax.experimental.pallas import tpu as pltpu
from jax.sharding import PartitionSpec as P

EPSILON = 1e-05


def merged_2(value, axis, combine):
    everything = jax.tree.map(lambda part: lax.all_gather(part, axis), value)
    first = jax.tree.map(lambda part: part[0], everything)

    def turn(k, so_far):
        return combine(so_far, jax.tree.map(lambda part: part[k], everything))

    return lax.fori_loop(1, lax.axis_size(axis), turn, first)


def merge_stats(earlier, follows):
    joint_max = jnp.maximum(earlier[0], follows[0])
    joint_sum = earlier[1] * jnp.exp(earlier[0] - joint_max) + follows[1] * jnp.exp(
        follows[0] - joint_max
    )
    return (joint_max, joint_sum, earlier[2] + follows[2])


def plain_body(gate_pre, up_pre, down_weight, residual, norm_gain, head_weight, targets):
    vocab_count = lax.axis_size("vocab")
    model_count = lax.axis_size("mp")
    model_index = lax.axis_index("mp")
    vocab_index = lax.axis_index("vocab")
    gated_units = (jax.nn.silu(gate_pre.astype(jnp.float32)) * up_pre.astype(jnp.float32)).astype(
        jnp.bfloat16
    )
    down_terms = lax.dot_general(
        lax.all_gather(gated_units, "vocab", axis=0, tiled=True),
        down_weight,
        (((1,), (1,)), ((), ())),
        preferred_element_type=jnp.float32,
    )
    own_rows = residual.shape[0]
    block_cols = down_weight.shape[0]
    grouped = down_terms.reshape(vocab_count, model_count, own_rows, block_cols)
    arrived = lax.all_to_all(
        lax.all_to_all(grouped, "vocab", split_axis=0, concat_axis=3, tiled=True),
        "mp",
        split_axis=1,
        concat_axis=0,
        tiled=True,
    )
    update = jnp.sum(arrived, axis=(0, 1))
    stream = (residual.astype(jnp.float32) + update).astype(jnp.bfloat16)
    stream = lax.optimization_barrier(stream)
    widened = stream.astype(jnp.float32)
    mean_square = jnp.mean(widened * widened, axis=1, keepdims=True)
    normed = (
        widened * lax.rsqrt(mean_square + EPSILON) * norm_gain.astype(jnp.float32)[None, :]
    ).astype(jnp.bfloat16)
    half_width = head_weight.shape[0]
    halves = lax.dynamic_slice_in_dim(
        lax.all_gather(normed, ("vocab", "mp"), axis=0, tiled=True),
        model_index * half_width,
        half_width,
        1,
    )
    logit_terms = jnp.dot(halves, head_weight, preferred_element_type=jnp.float32)
    logits = lax.psum_scatter(logit_terms, "mp", scatter_dimension=0, tiled=True)
    local_ids = targets - vocab_index * logits.shape[1]
    columns = lax.broadcasted_iota(jnp.int32, logits.shape, 1)
    chosen = jnp.sum(jnp.where(columns == local_ids[:, None], logits, 0.0), axis=1)
    row_top = jnp.max(logits, axis=1)
    exp_total = jnp.sum(jnp.exp(logits - row_top[:, None]), axis=1)
    merged = merged_2((row_top, exp_total, chosen), "vocab", merge_stats)
    return merged[2] - merged[0] - jnp.log(merged[1])


GATHER_CHUNKS = 7
MATRIX_SIDE = 256
LANES = 128


def diagonal(rows):
    return lax.broadcasted_iota(jnp.int32, (rows, LANES), 0) == lax.broadcasted_iota(
        jnp.int32, (rows, LANES), 1
    )


def to_lanes(column):
    rows = column.shape[0]
    spread = jnp.where(diagonal(rows), jnp.broadcast_to(column, (rows, LANES)), 0.0)
    return jnp.sum(spread, axis=0, keepdims=True)


def to_rows(lanes, rows):
    spread = jnp.where(diagonal(rows), jnp.broadcast_to(lanes, (rows, LANES)), 0.0)
    return jnp.sum(spread, axis=1, keepdims=True)


def kernel(
    V,
    M,
    targets_ref,
    gate_hbm,
    up_hbm,
    down_hbm,
    residual_hbm,
    gain_hbm,
    head_hbm,
    out_ref,
    gate,
    up,
    down,
    own_residual,
    gain,
    gain_rows,
    head,
    gated_in,
    gated_rows,
    residual_out,
    residual_in,
    residual_rows,
    update_out,
    update_in,
    stream_out,
    stream_in,
    square_in,
    logits_out,
    logits_in,
    stats_in,
    in_sem,
    down_sem,
    gated_send,
    gated_recv,
    residual_send,
    residual_recv,
    update_sem,
    stream_send,
    stream_recv,
    square_send,
    square_recv,
    logits_sem,
    stats_send,
    stats_recv,
):
    v = lax.axis_index("vocab")
    m = lax.axis_index("mp")
    other = 1 - m
    me = v * M + m
    N = V * M
    token_rows, width = gate.shape
    T = V * token_rows
    block_cols = down.shape[1]
    part_cols = block_cols // M
    chunks, _, chunk_cols = down.shape
    own_tokens = T // M
    vocab_cols = head.shape[0]
    half_owner = v // (V // M)

    def peer(i):
        return lax.rem(me + i, N)

    def coords(index):
        return {"vocab": index // M, "mp": lax.rem(index, M)}

    def remote(src, dst, send, recv, vocab, mp):
        return pltpu.make_async_remote_copy(
            src_ref=src,
            dst_ref=dst,
            send_sem=send,
            recv_sem=recv,
            device_id={"vocab": vocab, "mp": mp},
            device_id_type=pl.DeviceIdType.MESH,
        )

    barrier = pltpu.get_barrier_semaphore()
    for i in range(1, N):
        pl.semaphore_signal(
            barrier, inc=1, device_id=coords(peer(i)), device_id_type=pl.DeviceIdType.MESH
        )

    loads = [
        pltpu.make_async_copy(gate_hbm, gate, in_sem.at[0]),
        pltpu.make_async_copy(up_hbm, up, in_sem.at[1]),
        pltpu.make_async_copy(residual_hbm, own_residual, in_sem.at[2]),
        pltpu.make_async_copy(
            gain_hbm.at[pl.ds(pl.multiple_of(m * gain.shape[0], gain.shape[0]), gain.shape[0])],
            gain,
            in_sem.at[3],
        ),
        pltpu.make_async_copy(head_hbm, head, in_sem.at[4]),
    ]
    for load in loads[:3]:
        load.start()

    def down_copy(k):
        return pltpu.make_async_copy(
            down_hbm.at[:, pl.ds(pl.multiple_of(k * chunk_cols, chunk_cols), chunk_cols)],
            down.at[k],
            down_sem.at[k],
        )

    for k in range(chunks):
        down_copy(k).start()
    loads[4].start()
    loads[3].start()

    def gated_copy(a, i):
        to = lax.rem(v + i, V)
        return remote(
            gated_in.at[a, v], gated_in.at[a, v], gated_send.at[a, i], gated_recv.at[a, v], to, m
        )

    def gated_arrival(a, i):
        source = lax.rem(v + i, V)
        return remote(
            gated_in.at[a, source],
            gated_in.at[a, source],
            gated_send.at[a, i],
            gated_recv.at[a, source],
            source,
            m,
        )

    def residual_copy(i):
        to = peer(i)
        return remote(
            residual_out.at[to],
            residual_in.at[me],
            residual_send.at[i],
            residual_recv.at[me],
            to // M,
            lax.rem(to, M),
        )

    def residual_arrival(i):
        source = peer(i)
        return remote(
            residual_out.at[source],
            residual_in.at[source],
            residual_send.at[i],
            residual_recv.at[source],
            source // M,
            lax.rem(source, M),
        )

    loads[0].wait()
    loads[1].wait()
    for a in range(chunks):
        part = slice(a * chunk_cols, (a + 1) * chunk_cols)
        g = gate[:, part].astype(jnp.float32)
        u = up[:, part].astype(jnp.float32)
        gated_in[a, v] = (jax.nn.silu(g) * u).astype(jnp.bfloat16)
        if a == 0:
            pl.semaphore_wait(barrier, N - 1)
        for i in range(1, V):
            gated_copy(a, i).start()
    loads[2].wait()
    for n in range(N):
        residual_out[n] = own_residual[:, n * part_cols : (n + 1) * part_cols].astype(jnp.float32)
    residual_in[me] = residual_out[me]
    for i in range(1, N):
        residual_copy(i).start()

    def await_chunk(a):
        for i in range(1, V):
            gated_arrival(a, i).wait_recv()
        down_copy(a).wait()

    def token_chunk(a):
        for s in range(V):
            gated_rows[a % 2, s * token_rows : (s + 1) * token_rows, :] = gated_in[a, s].astype(
                jnp.float32
            )
        return gated_rows[a % 2].astype(jnp.bfloat16)

    def term(gated, a, which):
        rows = pl.ds(pl.multiple_of(which * part_cols, part_cols), part_cols)
        return lax.dot_general(
            gated,
            down[a, rows, :],
            (((1,), (1,)), ((), ())),
            preferred_element_type=jnp.float32,
        )

    theirs = jnp.zeros((T, part_cols), jnp.float32)
    own = theirs
    await_chunk(0)
    gated = token_chunk(0)
    for a in range(chunks - 2):
        theirs = theirs + term(gated, a, other)
        await_chunk(a + 1)
        following = token_chunk(a + 1)
        own = own + term(gated, a, m)
        gated = following
    last = chunks - 1
    theirs = theirs + term(gated, last - 1, other)
    await_chunk(last)
    following = token_chunk(last)
    update_out[...] = theirs + term(following, last, other)
    swap = remote(update_out, update_in, update_sem.at[0], update_sem.at[1], v, other)
    swap.start()
    own = own + term(gated, last - 1, m) + term(following, last, m)

    loads[3].wait()
    loads[4].wait()
    group = part_cols // LANES
    gains = gain[...].astype(jnp.float32)
    for j in range(V):
        for q in range(group):
            gain_rows[j, :, q * LANES : (q + 1) * LANES] = gains[
                j * group + q : j * group + q + 1
            ]
    for i in range(1, N):
        residual_arrival(i).wait_recv()
    for n in range(N):
        residual_rows[n : n + 1, :] = residual_in[n]
    swap.wait_recv()
    stream = (residual_rows[...] + (own + update_in[...])).astype(jnp.bfloat16)
    stream_out[...] = stream
    wide = stream.astype(jnp.float32)
    square_in[me] = to_lanes(jnp.sum(wide * wide, axis=1, keepdims=True))

    slot = lax.rem(v, V // M) * M + m

    def square_copy(i):
        to = peer(i)
        return remote(
            square_in.at[me],
            square_in.at[me],
            square_send.at[i],
            square_recv.at[me],
            to // M,
            lax.rem(to, M),
        )

    def square_arrival(i):
        source = peer(i)
        return remote(
            square_in.at[source],
            square_in.at[source],
            square_send.at[i],
            square_recv.at[source],
            source // M,
            lax.rem(source, M),
        )

    quarter = V // M

    def stream_copy(i, h):
        to = lax.rem(v + i, quarter) + h * quarter
        return remote(
            stream_out,
            stream_in.at[slot],
            stream_send.at[h * quarter + i],
            stream_recv.at[slot],
            to,
            half_owner,
        )

    def over_stream(act):
        for i in range(quarter):
            for h in range(M):
                if i:
                    act(stream_copy(i, h))
                else:

                    @pl.when(jnp.logical_or(h != half_owner, m != half_owner))
                    def _():
                        act(stream_copy(i, h))

    def stream_arrival(j):
        return remote(
            stream_out, stream_in.at[j], stream_send.at[0], stream_recv.at[j], v, other
        )

    for i in range(1, N):
        square_copy(i).start()
    over_stream(lambda copy: copy.start())

    @pl.when(m == half_owner)
    def _():
        stream_in[slot] = stream

    for i in range(1, N):
        square_arrival(i).wait_recv()
    squares = square_in[0]
    for n in range(1, N):
        squares = squares + square_in[n]
    mean_square = to_rows(squares, T) * (1.0 / (N * part_cols))
    scale = lax.rsqrt(mean_square + EPSILON)

    partial = jnp.zeros((T, vocab_cols), jnp.float32)
    for i in range(quarter):
        source = lax.rem(v + quarter - i, quarter)
        for c in range(M):
            j = source * M + c
            if i:
                stream_arrival(j).wait_recv()
            else:

                @pl.when(jnp.logical_or(m != half_owner, m != c))
                def _():
                    stream_arrival(j).wait_recv()

            normed = (stream_in[j].astype(jnp.float32) * scale * gain_rows[j]).astype(
                jnp.bfloat16
            )
            features = pl.ds(pl.multiple_of(j * part_cols, part_cols), part_cols)
            partial = partial + lax.dot_general(
                normed,
                head[:, features],
                (((1,), (1,)), ((), ())),
                preferred_element_type=jnp.float32,
            )

    for n in range(M):
        logits_out[n] = partial[n * own_tokens : (n + 1) * own_tokens, :]
    swap_logits = remote(
        logits_out.at[other], logits_in, logits_sem.at[0], logits_sem.at[1], v, other
    )
    swap_logits.start()
    row = lax.broadcasted_iota(jnp.int32, (own_tokens, vocab_cols), 0)
    wanted = jnp.zeros((own_tokens, vocab_cols), jnp.int32)
    for t in range(own_tokens):
        wanted = jnp.where(row == t, targets_ref[t], wanted)
    columns = lax.broadcasted_iota(jnp.int32, (own_tokens, vocab_cols), 1) + v * vocab_cols
    swap_logits.wait_recv()
    logits = logits_out[m] + logits_in[...]
    top = jnp.max(logits, axis=1, keepdims=True)
    total = jnp.sum(jnp.exp(logits - top), axis=1, keepdims=True)
    chosen = jnp.sum(jnp.where(columns == wanted, logits, 0.0), axis=1, keepdims=True)
    stats_in[v, :, 0:LANES] = to_lanes(top)
    stats_in[v, :, LANES : 2 * LANES] = to_lanes(total)
    stats_in[v, :, 2 * LANES : 3 * LANES] = to_lanes(chosen)

    def stats_copy(i):
        return remote(
            stats_in.at[v],
            stats_in.at[v],
            stats_send.at[i],
            stats_recv.at[v],
            lax.rem(v + i, V),
            m,
        )

    def stats_arrival(i):
        source = lax.rem(v + i, V)
        return remote(
            stats_in.at[source],
            stats_in.at[source],
            stats_send.at[i],
            stats_recv.at[source],
            source,
            m,
        )

    for i in range(1, V):
        stats_copy(i).start()
    for a in range(chunks):
        for i in range(1, V):
            gated_copy(a, i).wait_send()
    for i in range(1, N):
        residual_copy(i).wait_send()
        square_copy(i).wait_send()
    over_stream(lambda copy: copy.wait_send())

    swap.wait_send()
    swap_logits.wait_send()
    for i in range(1, V):
        stats_arrival(i).wait_recv()
    joint = stats_in[0, :, 0:LANES]
    for n in range(1, V):
        joint = jnp.maximum(joint, stats_in[n, :, 0:LANES])
    exp_total = jnp.zeros((1, LANES), jnp.float32)
    picked = jnp.zeros((1, LANES), jnp.float32)
    for n in range(V):
        exp_total = exp_total + stats_in[n, :, LANES : 2 * LANES] * jnp.exp(
            stats_in[n, :, 0:LANES] - joint
        )
        picked = picked + stats_in[n, :, 2 * LANES : 3 * LANES]
    out_ref[...] = picked - joint - jnp.log(exp_total)
    for i in range(1, V):
        stats_copy(i).wait_send()


def body(gate_pre, up_pre, down_weight, residual, norm_gain, head_weight, targets):
    V = lax.axis_size("vocab")
    M = lax.axis_size("mp")
    token_rows, width = gate_pre.shape
    block_cols = down_weight.shape[0]
    half_width, vocab_cols = head_weight.shape
    T = V * token_rows
    fits = (
        M == 2
        and V % M == 0
        and T <= LANES
        and T % 16 == 0
        and residual.shape[0] == 1
        and block_cols % (M * LANES) == 0
        and width % (GATHER_CHUNKS * MATRIX_SIDE) == 0
        and half_width % (16 * LANES) == 0
    )
    if not fits:
        return plain_body(
            gate_pre, up_pre, down_weight, residual, norm_gain, head_weight, targets
        )
    N = V * M
    part_cols = block_cols // M
    chunk_cols = width // GATHER_CHUNKS
    slots = V
    any_space = pl.BlockSpec(memory_space=pl.ANY)
    f32, bf16 = jnp.float32, jnp.bfloat16
    dma = pltpu.SemaphoreType.DMA
    result = pl.pallas_call(
        functools.partial(kernel, V, M),
        out_shape=jax.ShapeDtypeStruct((1, LANES), f32),
        in_specs=[pl.BlockSpec(memory_space=pltpu.SMEM)] + [any_space] * 6,
        out_specs=pl.BlockSpec(memory_space=pltpu.VMEM),
        scratch_shapes=[
            pltpu.VMEM((token_rows, width), bf16),
            pltpu.VMEM((token_rows, width), bf16),
            pltpu.VMEM((GATHER_CHUNKS, block_cols, chunk_cols), bf16),
            pltpu.VMEM(residual.shape, bf16),
            pltpu.VMEM((half_width // LANES, LANES), bf16),
            pltpu.VMEM((slots, 1, part_cols), f32),
            pltpu.VMEM((vocab_cols, half_width), bf16),
            pltpu.VMEM((GATHER_CHUNKS, V, token_rows, chunk_cols), bf16),
            pltpu.VMEM((2, T, chunk_cols), f32),
            pltpu.VMEM((N, 1, part_cols), f32),
            pltpu.VMEM((N, 1, part_cols), f32),
            pltpu.VMEM((T, part_cols), f32),
            pltpu.VMEM((T, part_cols), f32),
            pltpu.VMEM((T, part_cols), f32),
            pltpu.VMEM((T, part_cols), bf16),
            pltpu.VMEM((slots, T, part_cols), bf16),
            pltpu.VMEM((N, 1, LANES), f32),
            pltpu.VMEM((M, T // M, vocab_cols), f32),
            pltpu.VMEM((T // M, vocab_cols), f32),
            pltpu.VMEM((V, 1, 3 * LANES), f32),
            dma((5,)),
            dma((GATHER_CHUNKS,)),
            dma((GATHER_CHUNKS, V)),
            dma((GATHER_CHUNKS, V)),
            dma((N,)),
            dma((N,)),
            dma((2,)),
            dma((V,)),
            dma((slots,)),
            dma((N,)),
            dma((N,)),
            dma((2,)),
            dma((V,)),
            dma((V,)),
        ],
        compiler_params=pltpu.CompilerParams(
            collective_id=0, has_side_effects=True, vmem_limit_bytes=56 * 1024 * 1024
        ),
        name="scored_head",
    )(
        targets,
        gate_pre,
        up_pre,
        down_weight,
        residual,
        norm_gain.reshape(-1, LANES),
        head_weight.T,
    )
    return result[0, : targets.shape[0]]


def solution(mesh):
    return jax.shard_map(
        body,
        mesh=mesh,
        in_specs=(
            P(("groups", "vocab"), "mp"),
            P(("groups", "vocab"), "mp"),
            P("vocab", "mp"),
            P(("groups", "vocab", "mp"), None),
            P(),
            P("mp", "vocab"),
            P(("groups", "mp")),
        ),
        out_specs=P(("groups", "mp")),
        check_vma=False,
    )
```

```python
import functools

import jax
import jax.numpy as jnp
from jax import lax
from jax.experimental import pallas as pl
from jax.experimental.pallas import tpu as pltpu
from jax.sharding import PartitionSpec as P

EPSILON = 1e-05


def merged_2(value, axis, combine):
    everything = jax.tree.map(lambda part: lax.all_gather(part, axis), value)
    first = jax.tree.map(lambda part: part[0], everything)

    def turn(k, so_far):
        return combine(so_far, jax.tree.map(lambda part: part[k], everything))

    return lax.fori_loop(1, lax.axis_size(axis), turn, first)


def merge_stats(earlier, follows):
    joint_max = jnp.maximum(earlier[0], follows[0])
    joint_sum = earlier[1] * jnp.exp(earlier[0] - joint_max) + follows[1] * jnp.exp(
        follows[0] - joint_max
    )
    return (joint_max, joint_sum, earlier[2] + follows[2])


def plain_body(gate_pre, up_pre, down_weight, residual, norm_gain, head_weight, targets):
    vocab_count = lax.axis_size("vocab")
    model_count = lax.axis_size("mp")
    model_index = lax.axis_index("mp")
    vocab_index = lax.axis_index("vocab")
    gated_units = (jax.nn.silu(gate_pre.astype(jnp.float32)) * up_pre.astype(jnp.float32)).astype(
        jnp.bfloat16
    )
    down_terms = lax.dot_general(
        lax.all_gather(gated_units, "vocab", axis=0, tiled=True),
        down_weight,
        (((1,), (1,)), ((), ())),
        preferred_element_type=jnp.float32,
    )
    own_rows = residual.shape[0]
    block_cols = down_weight.shape[0]
    grouped = down_terms.reshape(vocab_count, model_count, own_rows, block_cols)
    arrived = lax.all_to_all(
        lax.all_to_all(grouped, "vocab", split_axis=0, concat_axis=3, tiled=True),
        "mp",
        split_axis=1,
        concat_axis=0,
        tiled=True,
    )
    update = jnp.sum(arrived, axis=(0, 1))
    stream = (residual.astype(jnp.float32) + update).astype(jnp.bfloat16)
    stream = lax.optimization_barrier(stream)
    widened = stream.astype(jnp.float32)
    mean_square = jnp.mean(widened * widened, axis=1, keepdims=True)
    normed = (
        widened * lax.rsqrt(mean_square + EPSILON) * norm_gain.astype(jnp.float32)[None, :]
    ).astype(jnp.bfloat16)
    half_width = head_weight.shape[0]
    halves = lax.dynamic_slice_in_dim(
        lax.all_gather(normed, ("vocab", "mp"), axis=0, tiled=True),
        model_index * half_width,
        half_width,
        1,
    )
    logit_terms = jnp.dot(halves, head_weight, preferred_element_type=jnp.float32)
    logits = lax.psum_scatter(logit_terms, "mp", scatter_dimension=0, tiled=True)
    local_ids = targets - vocab_index * logits.shape[1]
    columns = lax.broadcasted_iota(jnp.int32, logits.shape, 1)
    chosen = jnp.sum(jnp.where(columns == local_ids[:, None], logits, 0.0), axis=1)
    row_top = jnp.max(logits, axis=1)
    exp_total = jnp.sum(jnp.exp(logits - row_top[:, None]), axis=1)
    merged = merged_2((row_top, exp_total, chosen), "vocab", merge_stats)
    return merged[2] - merged[0] - jnp.log(merged[1])


GATHER_CHUNKS = 7
MATRIX_SIDE = 256
LANES = 128


def diagonal(rows):
    return lax.broadcasted_iota(jnp.int32, (rows, LANES), 0) == lax.broadcasted_iota(
        jnp.int32, (rows, LANES), 1
    )


def to_lanes(column):
    rows = column.shape[0]
    spread = jnp.where(diagonal(rows), jnp.broadcast_to(column, (rows, LANES)), 0.0)
    return jnp.sum(spread, axis=0, keepdims=True)


def to_rows(lanes, rows):
    spread = jnp.where(diagonal(rows), jnp.broadcast_to(lanes, (rows, LANES)), 0.0)
    return jnp.sum(spread, axis=1, keepdims=True)


def kernel(
    V,
    M,
    targets_ref,
    gate_hbm,
    up_hbm,
    down_hbm,
    residual_hbm,
    gain_hbm,
    head_hbm,
    out_ref,
    gate,
    up,
    down,
    own_residual,
    gain,
    gain_rows,
    head,
    gated_in,
    gated_rows,
    residual_out,
    residual_in,
    residual_rows,
    update_out,
    update_in,
    stream_out,
    stream_in,
    square_in,
    logits_out,
    logits_in,
    stats_in,
    in_sem,
    down_sem,
    gated_send,
    gated_recv,
    residual_send,
    residual_recv,
    update_sem,
    stream_send,
    stream_recv,
    square_send,
    square_recv,
    logits_sem,
    stats_send,
    stats_recv,
):
    v = lax.axis_index("vocab")
    m = lax.axis_index("mp")
    other = 1 - m
    me = v * M + m
    N = V * M
    token_rows, width = gate.shape
    T = V * token_rows
    block_cols = down.shape[1]
    part_cols = block_cols // M
    chunks, _, chunk_cols = down.shape
    own_tokens = T // M
    vocab_cols = head.shape[0]
    half_owner = v // (V // M)

    def peer(i):
        return lax.rem(me + i, N)

    def coords(index):
        return {"vocab": index // M, "mp": lax.rem(index, M)}

    def remote(src, dst, send, recv, vocab, mp):
        return pltpu.make_async_remote_copy(
            src_ref=src,
            dst_ref=dst,
            send_sem=send,
            recv_sem=recv,
            device_id={"vocab": vocab, "mp": mp},
            device_id_type=pl.DeviceIdType.MESH,
        )

    loads = [
        pltpu.make_async_copy(gate_hbm, gate, in_sem.at[0]),
        pltpu.make_async_copy(up_hbm, up, in_sem.at[1]),
        pltpu.make_async_copy(residual_hbm, own_residual, in_sem.at[2]),
        pltpu.make_async_copy(
            gain_hbm.at[pl.ds(pl.multiple_of(m * gain.shape[0], gain.shape[0]), gain.shape[0])],
            gain,
            in_sem.at[3],
        ),
        pltpu.make_async_copy(head_hbm, head, in_sem.at[4]),
    ]
    for load in loads[:3]:
        load.start()

    barrier = pltpu.get_barrier_semaphore()
    for i in range(1, N):
        pl.semaphore_signal(
            barrier, inc=1, device_id=coords(peer(i)), device_id_type=pl.DeviceIdType.MESH
        )

    def down_copy(k):
        return pltpu.make_async_copy(
            down_hbm.at[:, pl.ds(pl.multiple_of(k * chunk_cols, chunk_cols), chunk_cols)],
            down.at[k],
            down_sem.at[k],
        )

    for k in range(chunks):
        down_copy(k).start()
    loads[4].start()
    loads[3].start()

    def gated_copy(a, i):
        to = lax.rem(v + i, V)
        return remote(
            gated_in.at[a, v], gated_in.at[a, v], gated_send.at[a, i], gated_recv.at[a, v], to, m
        )

    def gated_arrival(a, i):
        source = lax.rem(v + i, V)
        return remote(
            gated_in.at[a, source],
            gated_in.at[a, source],
            gated_send.at[a, i],
            gated_recv.at[a, source],
            source,
            m,
        )

    def residual_copy(i):
        to = peer(i)
        return remote(
            residual_out.at[to],
            residual_in.at[me],
            residual_send.at[i],
            residual_recv.at[me],
            to // M,
            lax.rem(to, M),
        )

    def residual_arrival(i):
        source = peer(i)
        return remote(
            residual_out.at[source],
            residual_in.at[source],
            residual_send.at[i],
            residual_recv.at[source],
            source // M,
            lax.rem(source, M),
        )

    loads[0].wait()
    loads[1].wait()
    for a in range(chunks):
        part = slice(a * chunk_cols, (a + 1) * chunk_cols)
        g = gate[:, part].astype(jnp.float32)
        u = up[:, part].astype(jnp.float32)
        gated_in[a, v] = (jax.nn.silu(g) * u).astype(jnp.bfloat16)
        if a == 0:
            pl.semaphore_wait(barrier, N - 1)
        for i in range(1, V):
            gated_copy(a, i).start()
    loads[2].wait()
    for n in range(N):
        residual_out[n] = own_residual[:, n * part_cols : (n + 1) * part_cols].astype(jnp.float32)
    residual_in[me] = residual_out[me]
    for i in range(1, N):
        residual_copy(i).start()

    def await_chunk(a):
        for i in range(1, V):
            gated_arrival(a, i).wait_recv()
        down_copy(a).wait()

    def token_chunk(a):
        for s in range(V):
            gated_rows[a % 2, s * token_rows : (s + 1) * token_rows, :] = gated_in[a, s].astype(
                jnp.float32
            )
        return gated_rows[a % 2].astype(jnp.bfloat16)

    def term(gated, a, which):
        rows = pl.ds(pl.multiple_of(which * part_cols, part_cols), part_cols)
        return lax.dot_general(
            gated,
            down[a, rows, :],
            (((1,), (1,)), ((), ())),
            preferred_element_type=jnp.float32,
        )

    theirs = jnp.zeros((T, part_cols), jnp.float32)
    own = theirs
    await_chunk(0)
    gated = token_chunk(0)
    for a in range(chunks - 2):
        theirs = theirs + term(gated, a, other)
        await_chunk(a + 1)
        following = token_chunk(a + 1)
        own = own + term(gated, a, m)
        gated = following
    last = chunks - 1
    theirs = theirs + term(gated, last - 1, other)
    await_chunk(last)
    following = token_chunk(last)
    update_out[...] = theirs + term(following, last, other)
    swap = remote(update_out, update_in, update_sem.at[0], update_sem.at[1], v, other)
    swap.start()
    own = own + term(gated, last - 1, m) + term(following, last, m)

    loads[3].wait()
    loads[4].wait()
    group = part_cols // LANES
    gains = gain[...].astype(jnp.float32)
    for j in range(V):
        for q in range(group):
            gain_rows[j, :, q * LANES : (q + 1) * LANES] = gains[
                j * group + q : j * group + q + 1
            ]
    for i in range(1, N):
        residual_arrival(i).wait_recv()
    for n in range(N):
        residual_rows[n : n + 1, :] = residual_in[n]
    swap.wait_recv()
    stream = (residual_rows[...] + (own + update_in[...])).astype(jnp.bfloat16)
    stream_out[...] = stream
    wide = stream.astype(jnp.float32)
    square_in[me] = to_lanes(jnp.sum(wide * wide, axis=1, keepdims=True))

    slot = lax.rem(v, V // M) * M + m

    def square_copy(i):
        to = peer(i)
        return remote(
            square_in.at[me],
            square_in.at[me],
            square_send.at[i],
            square_recv.at[me],
            to // M,
            lax.rem(to, M),
        )

    def square_arrival(i):
        source = peer(i)
        return remote(
            square_in.at[source],
            square_in.at[source],
            square_send.at[i],
            square_recv.at[source],
            source // M,
            lax.rem(source, M),
        )

    quarter = V // M

    def stream_copy(i, h):
        to = lax.rem(v + i, quarter) + h * quarter
        return remote(
            stream_out,
            stream_in.at[slot],
            stream_send.at[h * quarter + i],
            stream_recv.at[slot],
            to,
            half_owner,
        )

    def over_stream(act):
        for i in range(quarter):
            for h in range(M):
                if i:
                    act(stream_copy(i, h))
                else:

                    @pl.when(jnp.logical_or(h != half_owner, m != half_owner))
                    def _():
                        act(stream_copy(i, h))

    def stream_arrival(j):
        return remote(
            stream_out, stream_in.at[j], stream_send.at[0], stream_recv.at[j], v, other
        )

    for i in range(1, N):
        square_copy(i).start()
    over_stream(lambda copy: copy.start())

    @pl.when(m == half_owner)
    def _():
        stream_in[slot] = stream

    for i in range(1, N):
        square_arrival(i).wait_recv()
    squares = square_in[0]
    for n in range(1, N):
        squares = squares + square_in[n]
    mean_square = to_rows(squares, T) * (1.0 / (N * part_cols))
    scale = lax.rsqrt(mean_square + EPSILON)

    partial = jnp.zeros((T, vocab_cols), jnp.float32)
    for i in range(quarter):
        source = lax.rem(v + quarter - i, quarter)
        for c in range(M):
            j = source * M + c
            if i:
                stream_arrival(j).wait_recv()
            else:

                @pl.when(jnp.logical_or(m != half_owner, m != c))
                def _():
                    stream_arrival(j).wait_recv()

            normed = (stream_in[j].astype(jnp.float32) * scale * gain_rows[j]).astype(
                jnp.bfloat16
            )
            features = pl.ds(pl.multiple_of(j * part_cols, part_cols), part_cols)
            partial = partial + lax.dot_general(
                normed,
                head[:, features],
                (((1,), (1,)), ((), ())),
                preferred_element_type=jnp.float32,
            )

    for n in range(M):
        logits_out[n] = partial[n * own_tokens : (n + 1) * own_tokens, :]
    swap_logits = remote(
        logits_out.at[other], logits_in, logits_sem.at[0], logits_sem.at[1], v, other
    )
    swap_logits.start()
    row = lax.broadcasted_iota(jnp.int32, (own_tokens, vocab_cols), 0)
    wanted = jnp.zeros((own_tokens, vocab_cols), jnp.int32)
    for t in range(own_tokens):
        wanted = jnp.where(row == t, targets_ref[t], wanted)
    columns = lax.broadcasted_iota(jnp.int32, (own_tokens, vocab_cols), 1) + v * vocab_cols
    swap_logits.wait_recv()
    logits = logits_out[m] + logits_in[...]
    top = jnp.max(logits, axis=1, keepdims=True)
    total = jnp.sum(jnp.exp(logits - top), axis=1, keepdims=True)
    chosen = jnp.sum(jnp.where(columns == wanted, logits, 0.0), axis=1, keepdims=True)
    stats_in[v, :, 0:LANES] = to_lanes(top)
    stats_in[v, :, LANES : 2 * LANES] = to_lanes(total)
    stats_in[v, :, 2 * LANES : 3 * LANES] = to_lanes(chosen)

    def stats_copy(i):
        return remote(
            stats_in.at[v],
            stats_in.at[v],
            stats_send.at[i],
            stats_recv.at[v],
            lax.rem(v + i, V),
            m,
        )

    def stats_arrival(i):
        source = lax.rem(v + i, V)
        return remote(
            stats_in.at[source],
            stats_in.at[source],
            stats_send.at[i],
            stats_recv.at[source],
            source,
            m,
        )

    for i in range(1, V):
        stats_copy(i).start()
    for a in range(chunks):
        for i in range(1, V):
            gated_copy(a, i).wait_send()
    for i in range(1, N):
        residual_copy(i).wait_send()
        square_copy(i).wait_send()
    over_stream(lambda copy: copy.wait_send())

    swap.wait_send()
    swap_logits.wait_send()
    for i in range(1, V):
        stats_arrival(i).wait_recv()
    joint = stats_in[0, :, 0:LANES]
    for n in range(1, V):
        joint = jnp.maximum(joint, stats_in[n, :, 0:LANES])
    exp_total = jnp.zeros((1, LANES), jnp.float32)
    picked = jnp.zeros((1, LANES), jnp.float32)
    for n in range(V):
        exp_total = exp_total + stats_in[n, :, LANES : 2 * LANES] * jnp.exp(
            stats_in[n, :, 0:LANES] - joint
        )
        picked = picked + stats_in[n, :, 2 * LANES : 3 * LANES]
    out_ref[...] = picked - joint - jnp.log(exp_total)
    for i in range(1, V):
        stats_copy(i).wait_send()


def body(gate_pre, up_pre, down_weight, residual, norm_gain, head_weight, targets):
    V = lax.axis_size("vocab")
    M = lax.axis_size("mp")
    token_rows, width = gate_pre.shape
    block_cols = down_weight.shape[0]
    half_width, vocab_cols = head_weight.shape
    T = V * token_rows
    fits = (
        M == 2
        and V % M == 0
        and T <= LANES
        and T % 16 == 0
        and residual.shape[0] == 1
        and block_cols % (M * LANES) == 0
        and width % (GATHER_CHUNKS * MATRIX_SIDE) == 0
        and half_width % (16 * LANES) == 0
    )
    if not fits:
        return plain_body(
            gate_pre, up_pre, down_weight, residual, norm_gain, head_weight, targets
        )
    N = V * M
    part_cols = block_cols // M
    chunk_cols = width // GATHER_CHUNKS
    slots = V
    any_space = pl.BlockSpec(memory_space=pl.ANY)
    f32, bf16 = jnp.float32, jnp.bfloat16
    dma = pltpu.SemaphoreType.DMA
    result = pl.pallas_call(
        functools.partial(kernel, V, M),
        out_shape=jax.ShapeDtypeStruct((1, LANES), f32),
        in_specs=[pl.BlockSpec(memory_space=pltpu.SMEM)] + [any_space] * 6,
        out_specs=pl.BlockSpec(memory_space=pltpu.VMEM),
        scratch_shapes=[
            pltpu.VMEM((token_rows, width), bf16),
            pltpu.VMEM((token_rows, width), bf16),
            pltpu.VMEM((GATHER_CHUNKS, block_cols, chunk_cols), bf16),
            pltpu.VMEM(residual.shape, bf16),
            pltpu.VMEM((half_width // LANES, LANES), bf16),
            pltpu.VMEM((slots, 1, part_cols), f32),
            pltpu.VMEM((vocab_cols, half_width), bf16),
            pltpu.VMEM((GATHER_CHUNKS, V, token_rows, chunk_cols), bf16),
            pltpu.VMEM((2, T, chunk_cols), f32),
            pltpu.VMEM((N, 1, part_cols), f32),
            pltpu.VMEM((N, 1, part_cols), f32),
            pltpu.VMEM((T, part_cols), f32),
            pltpu.VMEM((T, part_cols), f32),
            pltpu.VMEM((T, part_cols), f32),
            pltpu.VMEM((T, part_cols), bf16),
            pltpu.VMEM((slots, T, part_cols), bf16),
            pltpu.VMEM((N, 1, LANES), f32),
            pltpu.VMEM((M, T // M, vocab_cols), f32),
            pltpu.VMEM((T // M, vocab_cols), f32),
            pltpu.VMEM((V, 1, 3 * LANES), f32),
            dma((5,)),
            dma((GATHER_CHUNKS,)),
            dma((GATHER_CHUNKS, V)),
            dma((GATHER_CHUNKS, V)),
            dma((N,)),
            dma((N,)),
            dma((2,)),
            dma((V,)),
            dma((slots,)),
            dma((N,)),
            dma((N,)),
            dma((2,)),
            dma((V,)),
            dma((V,)),
        ],
        compiler_params=pltpu.CompilerParams(
            collective_id=0, has_side_effects=True, vmem_limit_bytes=56 * 1024 * 1024
        ),
        name="scored_head",
    )(
        targets,
        gate_pre,
        up_pre,
        down_weight,
        residual,
        norm_gain.reshape(-1, LANES),
        head_weight.T,
    )
    return result[0, : targets.shape[0]]


def solution(mesh):
    return jax.shard_map(
        body,
        mesh=mesh,
        in_specs=(
            P(("groups", "vocab"), "mp"),
            P(("groups", "vocab"), "mp"),
            P("vocab", "mp"),
            P(("groups", "vocab", "mp"), None),
            P(),
            P("mp", "vocab"),
            P(("groups", "mp")),
        ),
        out_specs=P(("groups", "mp")),
        check_vma=False,
    )
```
